512 devices in a mesh: seq: 64 (over x, z), head: 8 (over y, core).
Axes of the slice: x: 4, y: 4, z: 16, core: 2. Of those that a mesh axis runs over, the one named last changes fastest.
Arguments:
- tokens: bfloat16 [16384, 5376], P('seq', 'head'), may hold values from -6 to 6
- features: bfloat16 [512, 64, 1152], P('seq'), may hold values from -6 to 6
- starts: int32 [8], replicated, may hold values from 0 to 16128, as said below
- sources: int32 [8], replicated, may hold values from 0 to 56, as said below
- soft_gain: float32 [1152], replicated, may hold values from 0.25 to 1.75
- proj_weight: bfloat16 [1152, 5376], P(None, 'head'), may hold values from -0.1875 to 0.1875
- input_gain: float32 [5376], replicated, may hold values from 0.25 to 1.75
- query_weight: bfloat16 [5376, 2048], P('seq', 'head'), may hold values from -0.078125 to 0.078125
- key_weight: bfloat16 [5376, 1024], P('seq', 'head'), may hold values from -0.078125 to 0.078125
- value_weight: bfloat16 [5376, 1024], P('seq', 'head'), may hold values from -0.078125 to 0.078125
- query_gain: float32 [128], replicated, may hold values from 0.25 to 1.75
- key_gain: float32 [128], replicated, may hold values from 0.25 to 1.75
- out_weight: bfloat16 [2048, 5376], P('seq', 'head'), may hold values from -0.125 to 0.125
- post_gain: float32 [5376], P('head'), may hold values from 0.25 to 1.75
Outputs:
- layer_out: bfloat16 [16384, 5376], P('seq', 'head')
The draws below stay inside these ranges and needn't reach their ends.
Inputs may be any that keep to these rules, and one draw needn't show every extreme that they name: Image i takes positions starts[i] to starts[i] + 255; the spans are in increasing order of i, do not intersect, and each crosses one boundary between sequence shards. Distinct multiples of 8; image i's patches fill feature rows sources[i] * 8 onward.
All inputs are finite; a program needn't handle non-finite values.
Results may differ from the reference program's by a relative error of at most 0.012.
Values may be sent and summed in bfloat16 or wider, within the bound.
No kernel may reach another device: no remote copies, remote signals or barrier semaphores. Data moves between devices by JAX's collectives and lax.ppermute only.
A program may use at most 64 MiB of HBM per device.

```python
import jax
import jax.numpy as jnp
from jax import lax

D = 5376
HEADS = 16
KV_HEADS = 8
HEAD_DIM = 128
VIS = 1152
WINDOW = 1024
PATCH_SIDE = 64
POOL = 4
TOK_DEV = 256
IMG_TOK = 256
SHARDS_IMG = 8
IMAGES = 8
TOKENS = 16384
N_SEQ = 64


def draw_starts(key, part):
    key = jax.random.fold_in(key, 3)
    image_ids = jnp.arange(IMAGES, dtype=jnp.int32)
    boundary_shard = jnp.where(image_ids == IMAGES - 1, N_SEQ - 1, image_ids * SHARDS_IMG + 1).astype(jnp.int32)
    boundary = boundary_shard * TOK_DEV
    lowest = max(1, IMG_TOK - TOK_DEV)
    highest = min(IMG_TOK - 1, max(IMG_TOK // 2, lowest + IMG_TOK // 4))
    highest_each = jnp.minimum(boundary, highest).astype(jnp.int32)
    before = jax.random.randint(key, (IMAGES,), lowest, highest_each + 1, dtype=jnp.int32)
    return (boundary - before).astype(jnp.int32)


def draw_sources(key, part):
    shuffled = jax.random.permutation(jax.random.fold_in(key, 7), IMAGES)
    return shuffled.astype(jnp.int32) * SHARDS_IMG


def block_scale(stream_key, dims, split, least, largest):
    level = 1.0
    for dim, parts in split:
        steps = jax.random.uniform(jax.random.fold_in(jax.random.fold_in(stream_key, 6), dim), (parts,), jnp.float32, least / len(split), largest / len(split))
        level = level * jnp.repeat(jnp.exp(steps), dims[dim] // parts).reshape((-1,) + (1,) * (len(dims) - 1 - dim))
    return level


def noise(rng, shape, scale, limit, pieces=(), held_as=jnp.bfloat16):
    values = jax.random.normal(rng, shape, jnp.float32) * scale
    if len(pieces) > 0:
        values = block_scale(rng, shape, pieces, -0.22, 0.18) * values
    return jnp.clip(values, min=-limit, max=limit).astype(held_as)


def setup_inputs(seed: int = 0) -> dict:
    arg_keys = jax.random.split(jax.random.key(seed), 15)
    tokens = noise(arg_keys[0], (TOKENS, D), 1.0, 6.0, ((0, 64), (1, 8)))
    features = noise(arg_keys[1], (IMAGES * PATCH_SIDE, PATCH_SIDE, VIS), 1.0, 6.0, ((0, 64),))
    starts = draw_starts(jax.random.fold_in(arg_keys[14], 71), 0)
    sources = draw_sources(jax.random.fold_in(arg_keys[14], 71), 0)
    soft_gain = jnp.clip(1.0 + 0.15 * jax.random.normal(arg_keys[4], (VIS,), jnp.float32), 0.25, 1.75)
    proj_weight = noise(arg_keys[5], (VIS, D), VIS ** -0.5, 0.1875, ((1, 8),))
    input_gain = jnp.clip(1.0 + 0.15 * jax.random.normal(arg_keys[6], (D,), jnp.float32), 0.25, 1.75)
    query_weight = noise(arg_keys[7], (D, HEADS * HEAD_DIM), D ** -0.5, 0.078125, ((0, 64), (1, 8)))
    key_weight = noise(arg_keys[8], (D, KV_HEADS * HEAD_DIM), D ** -0.5, 0.078125, ((0, 64), (1, 8)))
    value_weight = noise(arg_keys[9], (D, KV_HEADS * HEAD_DIM), D ** -0.5, 0.078125, ((0, 64), (1, 8)))
    query_gain = jnp.clip(1.0 + 0.15 * jax.random.normal(arg_keys[10], (HEAD_DIM,), jnp.float32), 0.25, 1.75)
    key_gain = jnp.clip(1.0 + 0.15 * jax.random.normal(arg_keys[11], (HEAD_DIM,), jnp.float32), 0.25, 1.75)
    out_weight = noise(arg_keys[12], (HEADS * HEAD_DIM, D), (HEADS * HEAD_DIM) ** -0.5, 0.125, ((0, 64), (1, 8)))
    post_gain = jnp.clip(1.0 + 0.15 * jax.random.normal(arg_keys[13], (D,), jnp.float32), 0.25, 1.75)
    return dict(tokens=tokens, features=features, starts=starts, sources=sources, soft_gain=soft_gain, proj_weight=proj_weight, input_gain=input_gain, query_weight=query_weight, key_weight=key_weight, value_weight=value_weight, query_gain=query_gain, key_gain=key_gain, out_weight=out_weight, post_gain=post_gain)


EPSILON = 1e-06
QUERY_SCALE = 168.0 ** (-0.5)
ROPE_BASE = 10000.0

def rms_scale(inputs, scale_gain):
    return inputs * lax.rsqrt(lax.optimization_barrier(jnp.mean(inputs * inputs, axis=-1, keepdims=True)) + EPSILON) * scale_gain

def rotate(inputs, positions):
    half_dim = inputs.shape[-1] // 2
    frequency = ROPE_BASE ** (-jnp.arange(half_dim, dtype=jnp.float32) * 2.0 / inputs.shape[-1])
    angles = positions.astype(jnp.float32)[:, None] * frequency[None, :]
    cosine = jnp.cos(angles)[:, None, :]
    sine_part = jnp.sin(angles)[:, None, :]
    first_half = inputs[..., :half_dim]
    second = inputs[..., half_dim:]
    return jnp.concatenate([first_half * cosine - second * sine_part, second * cosine + first_half * sine_part], axis=-1)

def image_of(positions, starts):
    inside = (positions[:, None] >= starts[None, :]) & (positions[:, None] < starts[None, :] + IMG_TOK)
    labels = jnp.arange(1, starts.shape[0] + 1, dtype=jnp.int32)
    return lax.optimization_barrier(jnp.sum(jnp.where(inside, labels[None, :], 0), axis=1)).astype(jnp.int32) - 1

def allowed_keys(query_pos, key_pos, starts, total_rows):
    query_img = image_of(query_pos, starts)
    key_img = image_of(key_pos, starts)
    inside = (key_pos >= 0) & (key_pos < total_rows)
    in_window = query_pos[:, None] - key_pos[None, :] < WINDOW
    causal = key_pos[None, :] <= query_pos[:, None]
    same_image = (query_img[:, None] == key_img[None, :]) & (query_img[:, None] >= 0)
    return inside[None, :] & in_window & (causal | same_image)

def attend(queries, key_rows, values, allowed):
    scores = jnp.einsum('qgrd,kgd->grqk', queries.astype(jnp.float32), key_rows.astype(jnp.float32))
    scores = jnp.where(allowed[None, None], scores, -jnp.inf)
    row_max = lax.optimization_barrier(jnp.max(scores, axis=-1, keepdims=True))
    weights = jnp.exp(scores - row_max)
    row_sum = lax.optimization_barrier(jnp.sum(weights, axis=-1))
    rounded = lax.optimization_barrier(weights.astype(jnp.bfloat16)).astype(jnp.float32)
    mixed_heads = jnp.einsum('grqk,kgd->qgrd', rounded, values.astype(jnp.float32))
    return (mixed_heads / jnp.transpose(row_sum, (2, 0, 1))[..., None]).astype(jnp.bfloat16)

def reference(tokens, features, starts, sources, soft_gain, proj_weight, input_gain, query_weight, key_weight, value_weight, query_gain, key_gain, out_weight, post_gain):
    pooled_side = PATCH_SIDE // POOL
    patch_grid = features.reshape(IMAGES, pooled_side, POOL, pooled_side, POOL, VIS)
    pooled = lax.optimization_barrier(jnp.sum(patch_grid, axis=(2, 4), dtype=jnp.float32)).reshape(IMAGES * IMG_TOK, VIS) / (POOL * POOL)
    soft = rms_scale(pooled, soft_gain).astype(jnp.bfloat16)
    embedded = jnp.dot(soft, proj_weight, preferred_element_type=jnp.float32).astype(jnp.bfloat16)
    slot_first = jnp.arange(IMAGES, dtype=jnp.int32) * SHARDS_IMG
    slot_start = lax.optimization_barrier(jnp.sum(jnp.where(sources[None, :] == slot_first[:, None], starts[None, :], 0), axis=1)).astype(jnp.int32)
    targets = (slot_start[:, None] + jnp.arange(IMG_TOK, dtype=jnp.int32)[None, :]).reshape(-1)
    residual = tokens.at[targets].set(embedded)
    normed = rms_scale(residual.astype(jnp.float32), input_gain).astype(jnp.bfloat16)
    positions = jnp.arange(TOKENS, dtype=jnp.int32)
    group_size = HEADS // KV_HEADS
    query_sum = jnp.dot(normed, query_weight, preferred_element_type=jnp.float32).reshape(TOKENS, HEADS, HEAD_DIM)
    key_sum = jnp.dot(normed, key_weight, preferred_element_type=jnp.float32).reshape(TOKENS, KV_HEADS, HEAD_DIM)
    values = jnp.dot(normed, value_weight, preferred_element_type=jnp.float32).astype(jnp.bfloat16).reshape(TOKENS, KV_HEADS, HEAD_DIM)
    queries = (rotate(rms_scale(query_sum, query_gain), positions) * QUERY_SCALE).astype(jnp.bfloat16)
    queries = queries.reshape(TOKENS, KV_HEADS, group_size, HEAD_DIM)
    key_block = rotate(rms_scale(key_sum, key_gain), positions).astype(jnp.bfloat16)
    block_rows = 512
    span_rows = block_rows + WINDOW + IMG_TOK
    keys_padded = jnp.pad(key_block, ((WINDOW, IMG_TOK), (0, 0), (0, 0)))
    values_padded = jnp.pad(values, ((WINDOW, IMG_TOK), (0, 0), (0, 0)))

    def one_block(block_index):
        first_row = block_index * block_rows
        query_part = lax.dynamic_slice_in_dim(queries, first_row, block_rows, 0)
        key_part = lax.dynamic_slice_in_dim(keys_padded, first_row, span_rows, 0)
        value_part = lax.dynamic_slice_in_dim(values_padded, first_row, span_rows, 0)
        query_pos = first_row + jnp.arange(block_rows, dtype=jnp.int32)
        key_pos = first_row - WINDOW + jnp.arange(span_rows, dtype=jnp.int32)
        allowed = allowed_keys(query_pos, key_pos, starts, TOKENS)
        return attend(query_part, key_part, value_part, allowed).reshape(block_rows, HEADS * HEAD_DIM)
    attended = lax.map(one_block, jnp.arange(TOKENS // block_rows, dtype=jnp.int32)).reshape(TOKENS, HEADS * HEAD_DIM)
    projected = jnp.dot(attended, out_weight, preferred_element_type=jnp.float32)
    post = rms_scale(projected, post_gain)
    return (residual.astype(jnp.float32) + post).astype(jnp.bfloat16)
```

```python
import jax
import jax.numpy as jnp
from jax import lax
from jax.sharding import Mesh
from jax.sharding import PartitionSpec as P

D = 5376
HEAD_DIM = 128
WINDOW = 1024
PATCH_SIDE = 64
POOL = 4
IMG_TOK = 256
SEQ = ("x", "z")
HEAD = ("y", "core")


EPSILON = 1e-06
QUERY_SCALE = 168.0 ** (-0.5)
ROPE_BASE = 10000.0


def shifted(value, axis, steps):
    count = lax.axis_size(axis)
    leading, last = (max(0, -steps), min(count, count - steps))
    return lax.ppermute(value, axis, [(source, source + steps) for source in range(leading, last)])


def rms_scale(inputs, scale_gain):
    return (
        inputs * lax.rsqrt(jnp.mean(inputs * inputs, axis=-1, keepdims=True) + EPSILON) * scale_gain
    )


def rotate(inputs, positions):
    half_dim = inputs.shape[-1] // 2
    frequency = ROPE_BASE ** (-jnp.arange(half_dim, dtype=jnp.float32) * 2.0 / inputs.shape[-1])
    angles = positions.astype(jnp.float32)[:, None] * frequency[None, :]
    cosine = jnp.cos(angles)[:, None, :]
    sine_part = jnp.sin(angles)[:, None, :]
    first_half = inputs[..., :half_dim]
    second = inputs[..., half_dim:]
    return jnp.concatenate(
        [first_half * cosine - second * sine_part, second * cosine + first_half * sine_part],
        axis=-1,
    )


def image_of(positions, starts):
    inside = (positions[:, None] >= starts[None, :]) & (
        positions[:, None] < starts[None, :] + IMG_TOK
    )
    labels = jnp.arange(1, starts.shape[0] + 1, dtype=jnp.int32)
    return jnp.sum(jnp.where(inside, labels[None, :], 0), axis=1) - 1


def allowed_keys(query_pos, key_pos, starts, total_rows):
    query_img = image_of(query_pos, starts)
    key_img = image_of(key_pos, starts)
    inside = (key_pos >= 0) & (key_pos < total_rows)
    in_window = query_pos[:, None] - key_pos[None, :] < WINDOW
    causal = key_pos[None, :] <= query_pos[:, None]
    same_image = (query_img[:, None] == key_img[None, :]) & (query_img[:, None] >= 0)
    return inside[None, :] & in_window & (causal | same_image)


def attend(queries, key_rows, values, allowed):
    scores = jnp.einsum("qgrd,kgd->grqk", queries, key_rows, preferred_element_type=jnp.float32)
    scores = jnp.where(allowed[None, None], scores, -jnp.inf)
    row_max = jnp.max(scores, axis=-1, keepdims=True)
    weights = jnp.exp(scores - row_max)
    row_sum = jnp.sum(weights, axis=-1)
    mixed_heads = jnp.einsum(
        "grqk,kgd->qgrd", weights.astype(jnp.bfloat16), values, preferred_element_type=jnp.float32
    )
    return (mixed_heads / jnp.transpose(row_sum, (2, 0, 1))[..., None]).astype(jnp.bfloat16)


def exchange(value, axes, count):
    spread = jnp.broadcast_to(value[None], (count, *value.shape))
    return lax.all_to_all(spread, axes, 0, 0, tiled=True)


def body(
    tokens,
    features,
    starts,
    sources,
    soft_gain,
    proj_weight,
    input_gain,
    query_weight,
    key_weight,
    value_weight,
    query_gain,
    key_gain,
    out_weight,
    post_gain,
):
    tok_rows, width = tokens.shape
    x_count = lax.axis_size("x")
    z_count = lax.axis_size("z")
    head_count = lax.axis_size("y") * lax.axis_size("core")
    seq_count = x_count * z_count
    x_index = lax.axis_index("x")
    z_index = lax.axis_index("z")
    head_index = lax.axis_index(HEAD)
    seq_index = lax.axis_index(SEQ)
    total_rows = seq_count * tok_rows
    rows_in = query_weight.shape[0]
    rows_out = out_weight.shape[0]

    qkv_local = jnp.concatenate([query_weight, key_weight, value_weight], axis=1)
    qkv_x = lax.all_gather(qkv_local, "x", axis=0, tiled=True)
    qkv_zx = lax.all_gather(qkv_x, "z", axis=0, tiled=True)
    out_x = lax.all_gather(out_weight, "x", axis=0, tiled=True)
    out_zx = lax.all_gather(out_x, "z", axis=0, tiled=True)

    image_count = starts.shape[0]
    vis = features.shape[2]
    pooled_side = PATCH_SIDE // POOL
    pool_rows = features.shape[0] // POOL
    block_rows = pool_rows * pooled_side
    shards_each = pooled_side // pool_rows
    patch_grid = features.reshape(pool_rows, POOL, pooled_side, POOL, vis)
    pooled = jnp.sum(patch_grid, axis=(1, 3), dtype=jnp.float32).reshape(block_rows, vis) / (
        POOL * POOL
    )
    soft = rms_scale(pooled, soft_gain).astype(jnp.bfloat16)
    vis_part = vis // head_count
    soft_part = lax.dynamic_slice_in_dim(soft, head_index * vis_part, vis_part, 1)
    soft_z = exchange(soft_part, "z", z_count).reshape(z_count * block_rows, vis_part)
    frame_pos = (
        (jnp.arange(x_count, dtype=jnp.int32)[:, None] * z_count + z_index) * tok_rows
        + jnp.arange(tok_rows, dtype=jnp.int32)[None, :]
    ).reshape(-1)
    frame_image = image_of(frame_pos, starts)
    row_base = sources // shards_each * (block_rows * shards_each) - starts
    image_ids = jnp.arange(image_count, dtype=jnp.int32)
    frame_row = jnp.sum(
        jnp.where(frame_image[:, None] == image_ids[None, :], row_base[None, :], 0), axis=1
    )
    frame_row = jnp.where(frame_image >= 0, frame_row + frame_pos, -1)
    here = x_index * (z_count * block_rows) + jnp.arange(z_count * block_rows, dtype=jnp.int32)
    chosen = (frame_row[:, None] == here[None, :]).astype(jnp.bfloat16)
    chosen = chosen.reshape(x_count, tok_rows, z_count * block_rows)
    frames = jnp.einsum("sk,xps->xkp", soft_z, chosen, preferred_element_type=jnp.float32)
    frames = lax.all_to_all(frames.astype(jnp.bfloat16), "x", 0, 0, tiled=True)
    mine = jnp.sum(frames.astype(jnp.float32), axis=0).astype(jnp.bfloat16)
    soft_rows = exchange(mine, HEAD, head_count).reshape(vis, tok_rows)
    embedded = lax.dot_general(
        soft_rows, proj_weight, (((0,), (0,)), ((), ())), preferred_element_type=jnp.float32
    ).astype(jnp.bfloat16)
    my_pos = seq_index * tok_rows + jnp.arange(tok_rows, dtype=jnp.int32)
    my_image = image_of(my_pos, starts)
    residual = jnp.where((my_image >= 0)[:, None], embedded, tokens)

    whole = exchange(residual, HEAD, head_count).astype(jnp.float32)
    mean_square = jnp.sum(whole * whole, axis=(0, 2), keepdims=True) / D
    gains = input_gain.reshape(head_count, 1, width)
    normed = (whole * lax.rsqrt(mean_square + EPSILON) * gains).astype(jnp.bfloat16)

    qkv_weight = (
        qkv_zx.reshape(z_count, x_count, rows_in, -1)
        .transpose(1, 0, 2, 3)
        .reshape(head_count, width, -1)
    )
    qkv = jnp.einsum("hqk,hkn->qn", normed, qkv_weight, preferred_element_type=jnp.float32)
    kv_local = key_weight.shape[1] // HEAD_DIM
    group_size = query_weight.shape[1] // key_weight.shape[1]
    q_width = query_weight.shape[1]
    k_width = key_weight.shape[1]
    query_sum = qkv[:, :q_width]
    key_sum = qkv[:, q_width : q_width + k_width]
    value_sum = qkv[:, q_width + k_width :]
    queries = (
        rotate(
            rms_scale(query_sum.reshape(tok_rows, kv_local * group_size, HEAD_DIM), query_gain),
            my_pos,
        )
        * QUERY_SCALE
    )
    queries = queries.astype(jnp.bfloat16).reshape(tok_rows, kv_local, group_size, HEAD_DIM)
    own_keys = (
        rotate(rms_scale(key_sum.reshape(tok_rows, kv_local, HEAD_DIM), key_gain), my_pos)
        .astype(jnp.bfloat16)
        .reshape(tok_rows, k_width)
    )
    own = jnp.concatenate([own_keys, value_sum.astype(jnp.bfloat16)], axis=1)
    past_count = WINDOW // tok_rows
    pieces = [shifted(own, SEQ, step) for step in range(past_count, 0, -1)]
    pieces += [own, shifted(own, SEQ, -1)]
    window = jnp.concatenate(pieces, axis=0)
    key_pos = (seq_index - past_count) * tok_rows + jnp.arange(window.shape[0], dtype=jnp.int32)
    allowed = allowed_keys(my_pos, key_pos, starts, total_rows)
    attended = attend(
        queries,
        window[:, :k_width].reshape(-1, kv_local, HEAD_DIM),
        window[:, k_width:].reshape(-1, kv_local, HEAD_DIM),
        allowed,
    )
    attended = attended.reshape(tok_rows, kv_local * group_size * HEAD_DIM)
    heads_all = exchange(attended, HEAD, head_count)
    heads_weight = (
        out_zx.reshape(z_count, x_count, rows_out, width)
        .transpose(1, 0, 2, 3)
        .reshape(head_count, q_width, width)
    )
    projected = jnp.einsum(
        "hqk,hkn->qn", heads_all, heads_weight, preferred_element_type=jnp.float32
    )
    squares = jnp.sum(exchange(jnp.sum(projected * projected, axis=1), HEAD, head_count), axis=0)
    post = projected * lax.rsqrt(squares[:, None] / D + EPSILON) * post_gain
    return (residual.astype(jnp.float32) + post).astype(jnp.bfloat16)


def solution(mesh):
    split = Mesh(mesh.devices.reshape(4, 16, 4, 2), ("x", "z", "y", "core"))
    return jax.shard_map(
        body,
        mesh=split,
        in_specs=(
            P(SEQ, HEAD),
            P(SEQ, None, None),
            P(),
            P(),
            P(),
            P(None, HEAD),
            P(),
            P(SEQ, HEAD),
            P(SEQ, HEAD),
            P(SEQ, HEAD),
            P(),
            P(),
            P(SEQ, HEAD),
            P(HEAD),
        ),
        out_specs=P(SEQ, HEAD),
        check_vma=False,
    )
```

```python
import jax
import jax.numpy as jnp
from jax import lax
from jax.experimental import pallas as pl
from jax.experimental.pallas import tpu as pltpu
from jax.sharding import Mesh
from jax.sharding import PartitionSpec as P

D = 5376
HEAD_DIM = 128
WINDOW = 1024
PATCH_SIDE = 64
POOL = 4
IMG_TOK = 256
Z = 16
ROWS_IN = 84
ROWS_OUT = 32
PAD_IN = 96
PAD_ALL = 144
WIDTH = 672

EPSILON = 1e-06
QUERY_SCALE = 168.0 ** (-0.5)
ROPE_BASE = 10000.0

GIVEN_SEQ = ("k", "a", "z")
GIVEN_HEAD = ("y", "core")
SEQ = ("k", "core", "z")
HEAD = ("y", "a")


def swapped(value):
    return lax.ppermute(value, ("a", "core"), [(0, 0), (1, 2), (2, 1), (3, 3)])


def from_half(value, flip):
    pairs = []
    for k in range(2):
        for a in range(2):
            for core in range(2):
                pairs.append(((k * 2 + a) * 2 + core, ((k ^ flip) * 2 + core) * 2 + a))
    return lax.ppermute(value, ("k", "a", "core"), pairs)


def shifted(value, steps):
    pairs = []
    for source in range(4 * Z):
        target = source + steps
        if 0 <= target < 4 * Z:
            place = [
                ((shard // (2 * Z)) * Z + shard % Z) * 2 + shard // Z % 2
                for shard in (source, target)
            ]
            pairs.append((place[0], place[1]))
    return lax.ppermute(value, ("k", "z", "core"), pairs)


def exchange(value, axes, count):
    spread = jnp.broadcast_to(value[None], (count, *value.shape))
    return lax.all_to_all(spread, axes, 0, 0, tiled=True)


def rms_scale(inputs, scale_gain):
    return (
        inputs * lax.rsqrt(jnp.mean(inputs * inputs, axis=-1, keepdims=True) + EPSILON) * scale_gain
    )


def image_of(positions, starts):
    inside = (positions[:, None] >= starts[None, :]) & (
        positions[:, None] < starts[None, :] + IMG_TOK
    )
    labels = jnp.arange(1, starts.shape[0] + 1, dtype=jnp.int32)
    return jnp.sum(jnp.where(inside, labels[None, :], 0), axis=1) - 1


def allowed_keys(query_pos, key_pos, starts, total_rows):
    query_img = image_of(query_pos, starts)
    key_img = image_of(key_pos, starts)
    inside = (key_pos >= 0) & (key_pos < total_rows)
    in_window = query_pos[:, None] - key_pos[None, :] < WINDOW
    causal = key_pos[None, :] <= query_pos[:, None]
    same_image = (query_img[:, None] == key_img[None, :]) & (query_img[:, None] >= 0)
    return inside[None, :] & in_window & (causal | same_image)


def attend(queries, key_rows, values, allowed):
    scores = jnp.einsum("qgrd,kgd->grqk", queries, key_rows, preferred_element_type=jnp.float32)
    scores = jnp.where(allowed[None, None], scores, -jnp.inf)
    row_max = jnp.max(scores, axis=-1, keepdims=True)
    weights = jnp.exp(scores - row_max)
    row_sum = jnp.sum(weights, axis=-1)
    mixed_heads = jnp.einsum(
        "grqk,kgd->qgrd", weights.astype(jnp.bfloat16), values, preferred_element_type=jnp.float32
    )
    return (mixed_heads / jnp.transpose(row_sum, (2, 0, 1))[..., None]).astype(jnp.bfloat16)


def add_part(whole_ref, gain_ref, weight_ref, block, start, squares):
    for shard in range(8):
        block[shard * ROWS_IN : (shard + 1) * ROWS_IN, :] = weight_ref[shard, 0, :ROWS_IN, :]
    part = whole_ref[0].astype(jnp.float32)
    scaled = (part * gain_ref[0]).astype(jnp.bfloat16)
    product = lax.dot_general(
        scaled, block[...], (((0,), (0,)), ((), ())), preferred_element_type=jnp.float32
    )
    return start + product, squares + jnp.sum(part * part, axis=0, keepdims=True)


def first_kernel(core_ref, whole_ref, gain_ref, weight_ref, total_ref, squares_ref, block):
    @pl.when(pl.program_id(0) == 0)
    def _():
        total_ref[...] = jnp.zeros_like(total_ref)
        squares_ref[...] = jnp.zeros_like(squares_ref)

    total_ref[...], squares_ref[...] = add_part(
        whole_ref, gain_ref, weight_ref, block, total_ref[...], squares_ref[...]
    )


def second_kernel(
    core_ref, whole_ref, gain_ref, weight_ref, start_ref, square_ref, cos_ref, sin_ref,
    query_gain_ref, key_gain_ref, query_ref, pair_ref, block, total, squares,
):
    step = pl.program_id(0)

    @pl.when(step == 0)
    def _():
        total[...] = start_ref[...]
        squares[...] = square_ref[...]

    total[...], squares[...] = add_part(
        whole_ref, gain_ref, weight_ref, block, total[...], squares[...]
    )

    @pl.when(step == pl.num_programs(0) - 1)
    def _():
        inverse = lax.rsqrt(squares[...] / D + EPSILON)
        inverse = jnp.transpose(jnp.broadcast_to(inverse, (HEAD_DIM, inverse.shape[1])))

        def head(index):
            return total[:, index * HEAD_DIM : (index + 1) * HEAD_DIM] * inverse

        def turned(rows, gain):
            mean_square = jnp.mean(rows * rows, axis=-1, keepdims=True)
            rows = rows * lax.rsqrt(mean_square + EPSILON) * gain
            return rows * cos_ref[...] + pltpu.roll(rows, HEAD_DIM // 2, 1) * sin_ref[...]

        for index in range(2):
            query_ref[:, index * HEAD_DIM : (index + 1) * HEAD_DIM] = (
                turned(head(index), query_gain_ref[...]) * QUERY_SCALE
            ).astype(jnp.bfloat16)
        pair_ref[:, :HEAD_DIM] = turned(head(2), key_gain_ref[...]).astype(jnp.bfloat16)
        pair_ref[:, HEAD_DIM:] = head(3).astype(jnp.bfloat16)


def own_block(step, core):
    return step // 2 * 4 + core[0] * 2 + step % 2


def other_block(step, core):
    return step // 2 * 4 + (1 - core[0]) * 2 + step % 2


def qkv_specs(block_of, width, rows):
    return [
        pl.BlockSpec((1, width, rows), lambda step, core: (block_of(step, core), 0, 0)),
        pl.BlockSpec((1, width, 1), lambda step, core: (block_of(step, core), 0, 0)),
        pl.BlockSpec((8, 1, PAD_IN, 512), lambda step, core: (step % 2, step // 2, 0, 0)),
    ]


def project_first(core, whole, gain, weights):
    count, width, rows = whole.shape
    fixed = lambda step, core: (0, 0)
    return pl.pallas_call(
        first_kernel,
        grid_spec=pltpu.PrefetchScalarGridSpec(
            num_scalar_prefetch=1,
            grid=(count // 2,),
            in_specs=qkv_specs(own_block, width, rows),
            out_specs=[pl.BlockSpec((rows, 512), fixed), pl.BlockSpec((1, rows), fixed)],
            scratch_shapes=[pltpu.VMEM((width, 512), jnp.bfloat16)],
        ),
        out_shape=[
            jax.ShapeDtypeStruct((rows, 512), jnp.float32),
            jax.ShapeDtypeStruct((1, rows), jnp.float32),
        ],
        compiler_params=pltpu.CompilerParams(vmem_limit_bytes=24 * 2**20),
        cost_estimate=pl.CostEstimate(
            flops=rows * 512 * D, bytes_accessed=5 * 2**20, transcendentals=0
        ),
    )(core, whole, gain, weights)


def project_second(
    core, whole, gain, weights, total, squares, cosine, sine, query_gain, key_gain
):
    count, width, rows = whole.shape
    fixed = lambda step, core: (0, 0)
    return pl.pallas_call(
        second_kernel,
        grid_spec=pltpu.PrefetchScalarGridSpec(
            num_scalar_prefetch=1,
            grid=(count // 2,),
            in_specs=qkv_specs(other_block, width, rows)
            + [
                pl.BlockSpec((rows, 512), fixed),
                pl.BlockSpec((1, rows), fixed),
                pl.BlockSpec((rows, HEAD_DIM), fixed),
                pl.BlockSpec((rows, HEAD_DIM), fixed),
                pl.BlockSpec((1, HEAD_DIM), fixed),
                pl.BlockSpec((1, HEAD_DIM), fixed),
            ],
            out_specs=[pl.BlockSpec((rows, 256), fixed), pl.BlockSpec((rows, 256), fixed)],
            scratch_shapes=[
                pltpu.VMEM((width, 512), jnp.bfloat16),
                pltpu.VMEM((rows, 512), jnp.float32),
                pltpu.VMEM((1, rows), jnp.float32),
            ],
        ),
        out_shape=[
            jax.ShapeDtypeStruct((rows, 256), jnp.bfloat16),
            jax.ShapeDtypeStruct((rows, 256), jnp.bfloat16),
        ],
        compiler_params=pltpu.CompilerParams(vmem_limit_bytes=24 * 2**20),
        cost_estimate=pl.CostEstimate(
            flops=rows * 512 * D, bytes_accessed=5 * 2**20, transcendentals=0
        ),
    )(
        core, whole, gain, weights, total, squares, cosine, sine,
        query_gain[None, :], key_gain[None, :],
    )


def out_kernel(
    core_ref, own_ref, other_ref, along_ref, across_ref, result_ref, squares_ref, total
):
    step = pl.program_id(0)

    @pl.when(step == 0)
    def _():
        total[...] = jnp.zeros_like(total)

    for heads_ref, weight_ref in ((own_ref, along_ref), (other_ref, across_ref)):
        left = weight_ref[:, 0, :ROWS_OUT, :].reshape(8 * ROWS_OUT, 512)
        right = weight_ref[:, 0, ROWS_OUT:, :]
        right = jnp.concatenate([right[:, :, :256], right[:, :, 256:]], axis=1)
        right = right.reshape(8 * ROWS_OUT, 256)
        heads = heads_ref[0]
        for first, part in ((0, left), (512, right)):
            total[first : first + part.shape[1], :] += lax.dot_general(
                part, heads, (((0,), (0,)), ((), ())), preferred_element_type=jnp.float32
            )

    @pl.when(step == pl.num_programs(0) - 1)
    def _():
        result = total[:WIDTH, :]
        result_ref[...] = result
        squares_ref[...] = jnp.sum(result * result, axis=0, keepdims=True)


def project_out(core, heads, along, across):
    count, depth, rows = heads.shape
    fixed = lambda step, core: (0, 0)
    weights = pl.BlockSpec(
        (8, 1, PAD_ALL - PAD_IN, 512), lambda step, core: (step % 2, step // 2, 2, 0)
    )
    return pl.pallas_call(
        out_kernel,
        grid_spec=pltpu.PrefetchScalarGridSpec(
            num_scalar_prefetch=1,
            grid=(count // 2,),
            in_specs=[
                pl.BlockSpec((1, depth, rows), lambda step, core: (own_block(step, core), 0, 0)),
                pl.BlockSpec((1, depth, rows), lambda step, core: (other_block(step, core), 0, 0)),
                weights,
                weights,
            ],
            out_specs=[pl.BlockSpec((WIDTH, rows), fixed), pl.BlockSpec((1, rows), fixed)],
            scratch_shapes=[pltpu.VMEM((768, rows), jnp.float32)],
        ),
        out_shape=[
            jax.ShapeDtypeStruct((WIDTH, rows), jnp.float32),
            jax.ShapeDtypeStruct((1, rows), jnp.float32),
        ],
        compiler_params=pltpu.CompilerParams(vmem_limit_bytes=24 * 2**20),
        cost_estimate=pl.CostEstimate(
            flops=2 * rows * 768 * 2048, bytes_accessed=5 * 2**20, transcendentals=0
        ),
    )(core, heads, heads, along, across)


def body(
    tokens,
    features,
    starts,
    sources,
    soft_gain,
    proj_weight,
    input_gain,
    query_weight,
    key_weight,
    value_weight,
    query_gain,
    key_gain,
    out_weight,
    post_gain,
):
    tok_rows, width = tokens.shape
    head_count = 8
    x_count = 4
    seq_count = x_count * Z
    core_index = lax.axis_index("core")
    z_index = lax.axis_index("z")
    seq_index = lax.axis_index(SEQ)
    total_rows = seq_count * tok_rows

    out_right = jnp.pad(out_weight[:, 512:], ((0, 0), (0, 768 - width)))
    local = jnp.concatenate(
        [
            jnp.pad(
                jnp.concatenate([query_weight, key_weight, value_weight], axis=1),
                ((0, PAD_IN - ROWS_IN), (0, 0)),
            ),
            out_weight[:, :512],
            jnp.concatenate([out_right[:16], out_right[16:]], axis=1),
        ],
        axis=0,
    )
    same_half = from_half(local, 0)
    other_half = from_half(local, 1)
    k_first = lax.axis_index("k") == 0
    both = jnp.stack(
        [
            jnp.where(k_first, same_half, other_half),
            jnp.where(k_first, other_half, same_half),
        ]
    )
    along = lax.all_gather(both, "z", axis=0)
    core = core_index.astype(jnp.int32)[None]

    image_count = starts.shape[0]
    vis = features.shape[2]
    pooled_side = PATCH_SIDE // POOL
    pool_rows = features.shape[0] // POOL
    block_rows = pool_rows * pooled_side
    shards_each = pooled_side // pool_rows
    patch_grid = features.reshape(pool_rows, POOL, pooled_side, POOL, vis)
    pooled = jnp.sum(patch_grid, axis=(1, 3), dtype=jnp.float32).reshape(block_rows, vis) / (
        POOL * POOL
    )
    soft = rms_scale(pooled, soft_gain).astype(jnp.bfloat16)
    vis_part = vis // head_count
    soft_part = lax.dynamic_slice_in_dim(
        soft, lax.axis_index(GIVEN_HEAD) * vis_part, vis_part, 1
    )
    soft_z = exchange(soft_part, "z", Z).reshape(Z * block_rows, vis_part)
    target = jnp.arange(8, dtype=jnp.int32)
    target_k, target_a, target_core = target // 4, target // 2 % 2, target % 2
    target_seq = (target_k * 2 + target_core) * Z + z_index
    frame_pos = (
        target_seq[:, None] * tok_rows + jnp.arange(tok_rows, dtype=jnp.int32)[None, :]
    ).reshape(-1)
    frame_image = image_of(frame_pos, starts)
    row_base = sources // shards_each * (block_rows * shards_each) - starts
    image_ids = jnp.arange(image_count, dtype=jnp.int32)
    frame_row = jnp.sum(
        jnp.where(frame_image[:, None] == image_ids[None, :], row_base[None, :], 0), axis=1
    )
    wanted = (frame_image >= 0) & jnp.repeat(target_a == core_index, tok_rows)
    frame_row = jnp.where(wanted, frame_row + frame_pos, -1)
    x_index = lax.axis_index(("k", "a"))
    here = x_index * (Z * block_rows) + jnp.arange(Z * block_rows, dtype=jnp.int32)
    chosen = (frame_row[:, None] == here[None, :]).astype(jnp.bfloat16)
    chosen = chosen.reshape(8, tok_rows, Z * block_rows)
    frames = jnp.einsum("sk,xps->xkp", soft_z, chosen, preferred_element_type=jnp.float32)
    frames = lax.all_to_all(
        frames.astype(jnp.bfloat16), ("k", "a", "core"), 0, 0, tiled=True
    )
    mine = jnp.sum(frames.astype(jnp.float32), axis=0).astype(jnp.bfloat16)
    soft_rows = exchange(mine, HEAD, head_count).reshape(vis, tok_rows)
    embedded = lax.dot_general(
        swapped(proj_weight), soft_rows, (((0,), (0,)), ((), ())),
        preferred_element_type=jnp.float32,
    ).astype(jnp.bfloat16)
    my_pos = seq_index * tok_rows + jnp.arange(tok_rows, dtype=jnp.int32)
    my_image = image_of(my_pos, starts)
    residual = jnp.where((my_image >= 0)[None, :], embedded, swapped(tokens).T)

    whole = exchange(residual, HEAD, head_count)
    along, residual = lax.optimization_barrier((along, residual))
    across = lax.ppermute(along, "core", [(0, 1), (1, 0)])
    half = HEAD_DIM // 2
    frequency = ROPE_BASE ** (-jnp.arange(half, dtype=jnp.float32) * 2.0 / HEAD_DIM)
    angles = my_pos.astype(jnp.float32)[:, None] * frequency[None, :]
    cosine, sine = jnp.cos(angles), jnp.sin(angles)
    gain_parts = input_gain.reshape(head_count, width, 1)
    total, row_squares = project_first(core, whole, gain_parts, along)
    queries, own = project_second(
        core,
        whole,
        gain_parts,
        across,
        total,
        row_squares,
        jnp.concatenate([cosine, cosine], axis=1),
        jnp.concatenate([-sine, sine], axis=1),
        query_gain,
        key_gain,
    )
    past_count = WINDOW // tok_rows
    pieces = [shifted(own, step) for step in range(past_count, 0, -1)]
    pieces += [own, shifted(own, -1)]
    window = jnp.concatenate(pieces, axis=0)
    key_pos = (seq_index - past_count) * tok_rows + jnp.arange(window.shape[0], dtype=jnp.int32)
    allowed = allowed_keys(my_pos, key_pos, starts, total_rows)
    attended = attend(
        queries.reshape(tok_rows, 1, 2, HEAD_DIM),
        window[:, :HEAD_DIM].reshape(-1, 1, HEAD_DIM),
        window[:, HEAD_DIM:].reshape(-1, 1, HEAD_DIM),
        allowed,
    )
    attended = attended.reshape(tok_rows, 2 * HEAD_DIM).T
    heads_all = exchange(attended, HEAD, head_count)
    projected, squares = project_out(core, heads_all, along, across)
    squares = jnp.sum(exchange(squares, HEAD, head_count), axis=0)
    gain = swapped(post_gain)[:, None]
    post = projected * lax.rsqrt(squares / D + EPSILON) * gain
    result = (residual.astype(jnp.float32) + post).astype(jnp.bfloat16)
    return swapped(result).T


def solution(mesh):
    split = Mesh(mesh.devices.reshape(2, 2, Z, 4, 2), ("k", "a", "z", "y", "core"))
    seq, head = GIVEN_SEQ, GIVEN_HEAD
    return jax.shard_map(
        body,
        mesh=split,
        in_specs=(
            P(seq, head),
            P(seq, None, None),
            P(),
            P(),
            P(),
            P(None, head),
            P(),
            P(seq, head),
            P(seq, head),
            P(seq, head),
            P(),
            P(),
            P(seq, head),
            P(head),
        ),
        out_specs=P(seq, head),
        check_vma=False,
    )
```

```python
import jax
import jax.numpy as jnp
from jax import lax
from jax.experimental import pallas as pl
from jax.experimental.pallas import tpu as pltpu
from jax.sharding import Mesh
from jax.sharding import PartitionSpec as P

D = 5376
HEAD_DIM = 128
WINDOW = 1024
PATCH_SIDE = 64
POOL = 4
IMG_TOK = 256
Z = 16
ROWS_IN = 84
ROWS_OUT = 32
PAD_IN = 96
PAD_ALL = 144
WIDTH = 672
UPPER = 512

EPSILON = 1e-06
QUERY_SCALE = 168.0 ** (-0.5)
ROPE_BASE = 10000.0

GIVEN_SEQ = ("k", "a", "z")
GIVEN_HEAD = ("y", "core")
SEQ = ("k", "core", "z")
HEAD = ("y", "a")


def swapped(value):
    return lax.ppermute(value, ("a", "core"), [(0, 0), (1, 2), (2, 1), (3, 3)])


def from_half(value, flip):
    pairs = []
    for k in range(2):
        for a in range(2):
            for core in range(2):
                pairs.append(((k * 2 + a) * 2 + core, ((k ^ flip) * 2 + core) * 2 + a))
    return lax.ppermute(value, ("k", "a", "core"), pairs)


def shifted(value, steps):
    pairs = []
    for source in range(4 * Z):
        target = source + steps
        if 0 <= target < 4 * Z:
            place = [
                ((shard // (2 * Z)) * Z + shard % Z) * 2 + shard // Z % 2
                for shard in (source, target)
            ]
            pairs.append((place[0], place[1]))
    return lax.ppermute(value, ("k", "z", "core"), pairs)


def exchange(value, axes, count, groups=None):
    spread = jnp.broadcast_to(value[None], (count, *value.shape))
    return lax.all_to_all(spread, axes, 0, 0, tiled=True, axis_index_groups=groups)


def rms_scale(inputs, scale_gain):
    return (
        inputs * lax.rsqrt(jnp.mean(inputs * inputs, axis=-1, keepdims=True) + EPSILON) * scale_gain
    )


def image_of(positions, starts):
    inside = (positions[:, None] >= starts[None, :]) & (
        positions[:, None] < starts[None, :] + IMG_TOK
    )
    labels = jnp.arange(1, starts.shape[0] + 1, dtype=jnp.int32)
    return jnp.sum(jnp.where(inside, labels[None, :], 0), axis=1) - 1


def allowed_keys(query_pos, key_pos, starts, total_rows):
    query_img = image_of(query_pos, starts)
    key_img = image_of(key_pos, starts)
    inside = (key_pos >= 0) & (key_pos < total_rows)
    in_window = query_pos[:, None] - key_pos[None, :] < WINDOW
    causal = key_pos[None, :] <= query_pos[:, None]
    same_image = (query_img[:, None] == key_img[None, :]) & (query_img[:, None] >= 0)
    return inside[None, :] & in_window & (causal | same_image)


def attend(queries, key_rows, values, allowed):
    scores = jnp.einsum("qgrd,kgd->grqk", queries, key_rows, preferred_element_type=jnp.float32)
    scores = jnp.where(allowed[None, None], scores, -jnp.inf)
    row_max = jnp.max(scores, axis=-1, keepdims=True)
    weights = jnp.exp(scores - row_max)
    row_sum = jnp.sum(weights, axis=-1)
    mixed_heads = jnp.einsum(
        "grqk,kgd->qgrd", weights.astype(jnp.bfloat16), values, preferred_element_type=jnp.float32
    )
    return (mixed_heads / jnp.transpose(row_sum, (2, 0, 1))[..., None]).astype(jnp.bfloat16)


def add_part(upper_ref, lower_ref, gain_ref, weight_ref, block, start, squares):
    for shard in range(8):
        block[shard * ROWS_IN : (shard + 1) * ROWS_IN, :] = weight_ref[shard, 0, :ROWS_IN, :]
    part = jnp.concatenate([upper_ref[0], lower_ref[0]], axis=0).astype(jnp.float32)
    scaled = (part * gain_ref[0]).astype(jnp.bfloat16)
    product = lax.dot_general(
        scaled, block[...], (((0,), (0,)), ((), ())), preferred_element_type=jnp.float32
    )
    return start + product, squares + jnp.sum(part * part, axis=0, keepdims=True)


def first_kernel(
    core_ref, upper_ref, lower_ref, gain_ref, weight_ref, total_ref, squares_ref, block
):
    @pl.when(pl.program_id(0) == 0)
    def _():
        total_ref[...] = jnp.zeros_like(total_ref)
        squares_ref[...] = jnp.zeros_like(squares_ref)

    total_ref[...], squares_ref[...] = add_part(
        upper_ref, lower_ref, gain_ref, weight_ref, block, total_ref[...], squares_ref[...]
    )


def second_kernel(
    core_ref, upper_ref, lower_ref, gain_ref, weight_ref, start_ref, square_ref, cos_ref, sin_ref,
    query_gain_ref, key_gain_ref, query_ref, pair_ref, block, total, squares,
):
    step = pl.program_id(0)

    @pl.when(step == 0)
    def _():
        total[...] = start_ref[...]
        squares[...] = square_ref[...]

    total[...], squares[...] = add_part(
        upper_ref, lower_ref, gain_ref, weight_ref, block, total[...], squares[...]
    )

    @pl.when(step == pl.num_programs(0) - 1)
    def _():
        inverse = lax.rsqrt(squares[...] / D + EPSILON)
        inverse = jnp.transpose(jnp.broadcast_to(inverse, (HEAD_DIM, inverse.shape[1])))

        def head(index):
            return total[:, index * HEAD_DIM : (index + 1) * HEAD_DIM] * inverse

        def turned(rows, gain):
            mean_square = jnp.mean(rows * rows, axis=-1, keepdims=True)
            rows = rows * lax.rsqrt(mean_square + EPSILON) * gain
            return rows * cos_ref[...] + pltpu.roll(rows, HEAD_DIM // 2, 1) * sin_ref[...]

        for index in range(2):
            query_ref[:, index * HEAD_DIM : (index + 1) * HEAD_DIM] = (
                turned(head(index), query_gain_ref[...]) * QUERY_SCALE
            ).astype(jnp.bfloat16)
        pair_ref[:, :HEAD_DIM] = turned(head(2), key_gain_ref[...]).astype(jnp.bfloat16)
        pair_ref[:, HEAD_DIM:] = head(3).astype(jnp.bfloat16)


def own_block(step, core):
    return step // 2 * 4 + core[0] * 2 + step % 2


def other_block(step, core):
    return step // 2 * 4 + (1 - core[0]) * 2 + step % 2


def qkv_specs(block_of, width, rows):
    def parts(height):
        return pl.BlockSpec((1, height, rows), lambda step, core: (block_of(step, core), 0, 0))

    return [
        parts(UPPER),
        parts(width - UPPER),
        pl.BlockSpec((1, width, 1), lambda step, core: (block_of(step, core), 0, 0)),
        pl.BlockSpec((8, 1, PAD_IN, 512), lambda step, core: (step % 2, step // 2, 0, 0)),
    ]


def project_first(core, upper, lower, gain, weights):
    count, _, rows = upper.shape
    width = WIDTH
    fixed = lambda step, core: (0, 0)
    return pl.pallas_call(
        first_kernel,
        grid_spec=pltpu.PrefetchScalarGridSpec(
            num_scalar_prefetch=1,
            grid=(count // 2,),
            in_specs=qkv_specs(own_block, width, rows),
            out_specs=[pl.BlockSpec((rows, 512), fixed), pl.BlockSpec((1, rows), fixed)],
            scratch_shapes=[pltpu.VMEM((width, 512), jnp.bfloat16)],
        ),
        out_shape=[
            jax.ShapeDtypeStruct((rows, 512), jnp.float32),
            jax.ShapeDtypeStruct((1, rows), jnp.float32),
        ],
        compiler_params=pltpu.CompilerParams(vmem_limit_bytes=24 * 2**20),
        cost_estimate=pl.CostEstimate(
            flops=rows * 512 * D, bytes_accessed=5 * 2**20, transcendentals=0
        ),
    )(core, upper, lower, gain, weights)


def project_second(
    core, upper, lower, gain, weights, total, squares, cosine, sine, query_gain, key_gain
):
    count, _, rows = upper.shape
    width = WIDTH
    fixed = lambda step, core: (0, 0)
    return pl.pallas_call(
        second_kernel,
        grid_spec=pltpu.PrefetchScalarGridSpec(
            num_scalar_prefetch=1,
            grid=(count // 2,),
            in_specs=qkv_specs(other_block, width, rows)
            + [
                pl.BlockSpec((rows, 512), fixed),
                pl.BlockSpec((1, rows), fixed),
                pl.BlockSpec((rows, HEAD_DIM), fixed),
                pl.BlockSpec((rows, HEAD_DIM), fixed),
                pl.BlockSpec((1, HEAD_DIM), fixed),
                pl.BlockSpec((1, HEAD_DIM), fixed),
            ],
            out_specs=[pl.BlockSpec((rows, 256), fixed), pl.BlockSpec((rows, 256), fixed)],
            scratch_shapes=[
                pltpu.VMEM((width, 512), jnp.bfloat16),
                pltpu.VMEM((rows, 512), jnp.float32),
                pltpu.VMEM((1, rows), jnp.float32),
            ],
        ),
        out_shape=[
            jax.ShapeDtypeStruct((rows, 256), jnp.bfloat16),
            jax.ShapeDtypeStruct((rows, 256), jnp.bfloat16),
        ],
        compiler_params=pltpu.CompilerParams(vmem_limit_bytes=24 * 2**20),
        cost_estimate=pl.CostEstimate(
            flops=rows * 512 * D, bytes_accessed=5 * 2**20, transcendentals=0
        ),
    )(
        core, upper, lower, gain, weights, total, squares, cosine, sine,
        query_gain[None, :], key_gain[None, :],
    )


def out_kernel(
    core_ref, own_ref, other_ref, along_ref, across_ref, result_ref, squares_ref, total
):
    step = pl.program_id(0)

    @pl.when(step == 0)
    def _():
        total[...] = jnp.zeros_like(total)

    for heads_ref, weight_ref in ((own_ref, along_ref), (other_ref, across_ref)):
        left = weight_ref[:, 0, :ROWS_OUT, :].reshape(8 * ROWS_OUT, 512)
        right = weight_ref[:, 0, ROWS_OUT:, :]
        right = jnp.concatenate([right[:, :, :256], right[:, :, 256:]], axis=1)
        right = right.reshape(8 * ROWS_OUT, 256)
        heads = heads_ref[0]
        for first, part in ((0, left), (512, right)):
            total[first : first + part.shape[1], :] += lax.dot_general(
                part, heads, (((0,), (0,)), ((), ())), preferred_element_type=jnp.float32
            )

    @pl.when(step == pl.num_programs(0) - 1)
    def _():
        result = total[:WIDTH, :]
        result_ref[...] = result
        squares_ref[...] = jnp.sum(result * result, axis=0, keepdims=True)


def project_out(core, heads, along, across):
    count, depth, rows = heads.shape
    fixed = lambda step, core: (0, 0)
    weights = pl.BlockSpec(
        (8, 1, PAD_ALL - PAD_IN, 512), lambda step, core: (step % 2, step // 2, 2, 0)
    )
    return pl.pallas_call(
        out_kernel,
        grid_spec=pltpu.PrefetchScalarGridSpec(
            num_scalar_prefetch=1,
            grid=(count // 2,),
            in_specs=[
                pl.BlockSpec((1, depth, rows), lambda step, core: (own_block(step, core), 0, 0)),
                pl.BlockSpec((1, depth, rows), lambda step, core: (other_block(step, core), 0, 0)),
                weights,
                weights,
            ],
            out_specs=[pl.BlockSpec((WIDTH, rows), fixed), pl.BlockSpec((1, rows), fixed)],
            scratch_shapes=[pltpu.VMEM((768, rows), jnp.float32)],
        ),
        out_shape=[
            jax.ShapeDtypeStruct((WIDTH, rows), jnp.float32),
            jax.ShapeDtypeStruct((1, rows), jnp.float32),
        ],
        compiler_params=pltpu.CompilerParams(vmem_limit_bytes=24 * 2**20),
        cost_estimate=pl.CostEstimate(
            flops=2 * rows * 768 * 2048, bytes_accessed=5 * 2**20, transcendentals=0
        ),
    )(core, heads, heads, along, across)


def body(
    tokens,
    features,
    starts,
    sources,
    soft_gain,
    proj_weight,
    input_gain,
    query_weight,
    key_weight,
    value_weight,
    query_gain,
    key_gain,
    out_weight,
    post_gain,
):
    tok_rows, width = tokens.shape
    head_count = 8
    x_count = 4
    seq_count = x_count * Z
    core_index = lax.axis_index("core")
    z_index = lax.axis_index("z")
    seq_index = lax.axis_index(SEQ)
    total_rows = seq_count * tok_rows

    out_right = jnp.pad(out_weight[:, 512:], ((0, 0), (0, 768 - width)))
    local = jnp.concatenate(
        [
            jnp.pad(
                jnp.concatenate([query_weight, key_weight, value_weight], axis=1),
                ((0, PAD_IN - ROWS_IN), (0, 0)),
            ),
            out_weight[:, :512],
            jnp.concatenate([out_right[:16], out_right[16:]], axis=1),
        ],
        axis=0,
    )
    same_half = from_half(local, 0)
    other_half = from_half(local, 1)
    k_first = lax.axis_index("k") == 0
    both = jnp.stack(
        [
            jnp.where(k_first, same_half, other_half),
            jnp.where(k_first, other_half, same_half),
        ]
    )
    along = lax.all_gather(both, "z", axis=0)
    core = core_index.astype(jnp.int32)[None]

    image_count = starts.shape[0]
    vis = features.shape[2]
    pooled_side = PATCH_SIDE // POOL
    pool_rows = features.shape[0] // POOL
    block_rows = pool_rows * pooled_side
    shards_each = pooled_side // pool_rows
    patch_grid = features.reshape(pool_rows, POOL, pooled_side, POOL, vis)
    pooled = jnp.sum(patch_grid, axis=(1, 3), dtype=jnp.float32).reshape(block_rows, vis) / (
        POOL * POOL
    )
    soft = rms_scale(pooled, soft_gain).astype(jnp.bfloat16)
    vis_part = vis // head_count
    soft_part = lax.dynamic_slice_in_dim(
        soft, lax.axis_index(GIVEN_HEAD) * vis_part, vis_part, 1
    )
    near_groups = [[4 * i + j for j in range(4)] for i in range(Z // 4)]
    far_groups = [[4 * i + j for i in range(Z // 4)] for j in range(4)]
    soft_z = exchange(soft_part, "z", 4, near_groups).reshape(4 * block_rows, vis_part)
    soft_z = exchange(soft_z, "z", 4, far_groups).reshape(Z * block_rows, vis_part)
    target = jnp.arange(8, dtype=jnp.int32)
    target_k, target_a, target_core = target // 4, target // 2 % 2, target % 2
    target_seq = (target_k * 2 + target_core) * Z + z_index
    frame_pos = (
        target_seq[:, None] * tok_rows + jnp.arange(tok_rows, dtype=jnp.int32)[None, :]
    ).reshape(-1)
    frame_image = image_of(frame_pos, starts)
    row_base = sources // shards_each * (block_rows * shards_each) - starts
    image_ids = jnp.arange(image_count, dtype=jnp.int32)
    frame_row = jnp.sum(
        jnp.where(frame_image[:, None] == image_ids[None, :], row_base[None, :], 0), axis=1
    )
    wanted = (frame_image >= 0) & jnp.repeat(target_a == core_index, tok_rows)
    frame_row = jnp.where(wanted, frame_row + frame_pos, -1)
    x_index = lax.axis_index(("k", "a"))
    here = x_index * (Z * block_rows) + jnp.arange(Z * block_rows, dtype=jnp.int32)
    chosen = (frame_row[:, None] == here[None, :]).astype(jnp.bfloat16)
    chosen = chosen.reshape(8, tok_rows, Z * block_rows)
    frames = jnp.einsum("sk,xps->xkp", soft_z, chosen, preferred_element_type=jnp.float32)
    frames = lax.all_to_all(
        frames.astype(jnp.bfloat16), ("k", "a", "core"), 0, 0, tiled=True
    )
    mine = jnp.sum(frames.astype(jnp.float32), axis=0).astype(jnp.bfloat16)
    soft_rows = exchange(mine, HEAD, head_count).reshape(vis, tok_rows)
    embedded = lax.dot_general(
        swapped(proj_weight), soft_rows, (((0,), (0,)), ((), ())),
        preferred_element_type=jnp.float32,
    ).astype(jnp.bfloat16)
    my_pos = seq_index * tok_rows + jnp.arange(tok_rows, dtype=jnp.int32)
    my_image = image_of(my_pos, starts)
    residual = jnp.where((my_image >= 0)[None, :], embedded, swapped(tokens).T)

    upper = exchange(residual[:UPPER], HEAD, head_count)
    lower = exchange(residual[UPPER:], HEAD, head_count)
    along, upper = lax.optimization_barrier((along, upper))
    across = lax.ppermute(along, "core", [(0, 1), (1, 0)])
    half = HEAD_DIM // 2
    frequency = ROPE_BASE ** (-jnp.arange(half, dtype=jnp.float32) * 2.0 / HEAD_DIM)
    angles = my_pos.astype(jnp.float32)[:, None] * frequency[None, :]
    cosine, sine = jnp.cos(angles), jnp.sin(angles)
    gain_parts = input_gain.reshape(head_count, width, 1)
    total, row_squares = project_first(core, upper, lower, gain_parts, along)
    queries, own = project_second(
        core,
        upper,
        lower,
        gain_parts,
        across,
        total,
        row_squares,
        jnp.concatenate([cosine, cosine], axis=1),
        jnp.concatenate([-sine, sine], axis=1),
        query_gain,
        key_gain,
    )
    past_count = WINDOW // tok_rows
    near = jnp.concatenate([shifted(own, 2), shifted(own, 1)], axis=0)
    window = jnp.concatenate([shifted(near, 2), near, own, shifted(own, -1)], axis=0)
    key_pos = (seq_index - past_count) * tok_rows + jnp.arange(window.shape[0], dtype=jnp.int32)
    allowed = allowed_keys(my_pos, key_pos, starts, total_rows)
    attended = attend(
        queries.reshape(tok_rows, 1, 2, HEAD_DIM),
        window[:, :HEAD_DIM].reshape(-1, 1, HEAD_DIM),
        window[:, HEAD_DIM:].reshape(-1, 1, HEAD_DIM),
        allowed,
    )
    attended = attended.reshape(tok_rows, 2 * HEAD_DIM).T
    attended, residual = lax.optimization_barrier((attended, residual))
    heads_all = exchange(attended, HEAD, head_count)
    projected, squares = project_out(core, heads_all, along, across)
    given_residual = swapped(residual).astype(jnp.float32)
    given = swapped(projected.astype(jnp.bfloat16)).astype(jnp.float32)
    all_squares = exchange(squares, ("a", "y", "core"), 16).reshape(8, 2, tok_rows)
    from_core = jnp.arange(2, dtype=jnp.int32) == lax.axis_index("a")
    squares = jnp.sum(jnp.where(from_core[None, :, None], all_squares, 0.0), axis=(0, 1))
    post = given * lax.rsqrt(squares[None, :] / D + EPSILON) * post_gain[:, None]
    return (given_residual + post).astype(jnp.bfloat16).T


def solution(mesh):
    split = Mesh(mesh.devices.reshape(2, 2, Z, 4, 2), ("k", "a", "z", "y", "core"))
    seq, head = GIVEN_SEQ, GIVEN_HEAD
    return jax.shard_map(
        body,
        mesh=split,
        in_specs=(
            P(seq, head),
            P(seq, None, None),
            P(),
            P(),
            P(),
            P(None, head),
            P(),
            P(seq, head),
            P(seq, head),
            P(seq, head),
            P(),
            P(),
            P(seq, head),
            P(head),
        ),
        out_specs=P(seq, head),
        check_vma=False,
    )
```

```python
import jax
import jax.numpy as jnp
from jax import lax
from jax.experimental import pallas as pl
from jax.experimental.pallas import tpu as pltpu
from jax.sharding import Mesh
from jax.sharding import PartitionSpec as P

D = 5376
HEAD_DIM = 128
WINDOW = 1024
PATCH_SIDE = 64
POOL = 4
IMG_TOK = 256
Z = 16
ROWS_IN = 84
ROWS_OUT = 32
PAD_IN = 96
PAD_ALL = 144
WIDTH = 672
UPPER = 512
VMEM = 56 * 2**20

EPSILON = 1e-06
QUERY_SCALE = 168.0 ** (-0.5)
ROPE_BASE = 10000.0

GIVEN_SEQ = ("k", "a", "z")
GIVEN_HEAD = ("y", "core")
SEQ = ("k", "core", "z")
HEAD = ("y", "a")


def swapped(value):
    return lax.ppermute(value, ("a", "core"), [(0, 0), (1, 2), (2, 1), (3, 3)])


def from_half(value, flip):
    pairs = []
    for k in range(2):
        for a in range(2):
            for core in range(2):
                pairs.append(((k * 2 + a) * 2 + core, ((k ^ flip) * 2 + core) * 2 + a))
    return lax.ppermute(value, ("k", "a", "core"), pairs)


def shifted(value, steps):
    pairs = []
    for source in range(4 * Z):
        target = source + steps
        if 0 <= target < 4 * Z:
            place = [
                ((shard // (2 * Z)) * Z + shard % Z) * 2 + shard // Z % 2
                for shard in (source, target)
            ]
            pairs.append((place[0], place[1]))
    return lax.ppermute(value, ("k", "z", "core"), pairs)


def exchange(value, axes, count, groups=None):
    spread = jnp.broadcast_to(value[None], (count, *value.shape))
    return lax.all_to_all(spread, axes, 0, 0, tiled=True, axis_index_groups=groups)


def rms_scale(inputs, scale_gain):
    return (
        inputs * lax.rsqrt(jnp.mean(inputs * inputs, axis=-1, keepdims=True) + EPSILON) * scale_gain
    )


def image_of(positions, starts):
    inside = (positions[:, None] >= starts[None, :]) & (
        positions[:, None] < starts[None, :] + IMG_TOK
    )
    labels = jnp.arange(1, starts.shape[0] + 1, dtype=jnp.int32)
    return jnp.sum(jnp.where(inside, labels[None, :], 0), axis=1) - 1


def allowed_keys(query_pos, key_pos, starts, total_rows):
    query_img = image_of(query_pos, starts)
    key_img = image_of(key_pos, starts)
    inside = (key_pos >= 0) & (key_pos < total_rows)
    in_window = query_pos[:, None] - key_pos[None, :] < WINDOW
    causal = key_pos[None, :] <= query_pos[:, None]
    same_image = (query_img[:, None] == key_img[None, :]) & (query_img[:, None] >= 0)
    return inside[None, :] & in_window & (causal | same_image)


def attend(queries, key_rows, values, allowed):
    scores = jnp.einsum("qgrd,kgd->grqk", queries, key_rows, preferred_element_type=jnp.float32)
    scores = jnp.where(allowed[None, None], scores, -jnp.inf)
    row_max = jnp.max(scores, axis=-1, keepdims=True)
    weights = jnp.exp(scores - row_max)
    row_sum = jnp.sum(weights, axis=-1)
    mixed_heads = jnp.einsum(
        "grqk,kgd->qgrd", weights.astype(jnp.bfloat16), values, preferred_element_type=jnp.float32
    )
    return (mixed_heads / jnp.transpose(row_sum, (2, 0, 1))[..., None]).astype(jnp.bfloat16)


def add_part(upper_ref, lower_ref, gain_ref, weight_ref, block, start, squares):
    for shard in range(8):
        block[shard * ROWS_IN : (shard + 1) * ROWS_IN, :] = weight_ref[shard, 0, :ROWS_IN, :]
    part = jnp.concatenate([upper_ref[0], lower_ref[0]], axis=0).astype(jnp.float32)
    scaled = (part * gain_ref[0]).astype(jnp.bfloat16)
    product = lax.dot_general(
        scaled, block[...], (((0,), (0,)), ((), ())), preferred_element_type=jnp.float32
    )
    return start + product, squares + jnp.sum(part * part, axis=0, keepdims=True)


def first_kernel(
    core_ref, upper_ref, lower_ref, gain_ref, weight_ref, total_ref, squares_ref, block
):
    @pl.when(pl.program_id(0) == 0)
    def _():
        total_ref[...] = jnp.zeros_like(total_ref)
        squares_ref[...] = jnp.zeros_like(squares_ref)

    total_ref[...], squares_ref[...] = add_part(
        upper_ref, lower_ref, gain_ref, weight_ref, block, total_ref[...], squares_ref[...]
    )


def second_kernel(
    core_ref, upper_ref, lower_ref, gain_ref, weight_ref, start_ref, square_ref, cos_ref, sin_ref,
    query_gain_ref, key_gain_ref, query_ref, pair_ref, block, total, squares,
):
    step = pl.program_id(0)

    @pl.when(step == 0)
    def _():
        total[...] = start_ref[...]
        squares[...] = square_ref[...]

    total[...], squares[...] = add_part(
        upper_ref, lower_ref, gain_ref, weight_ref, block, total[...], squares[...]
    )

    @pl.when(step == pl.num_programs(0) - 1)
    def _():
        inverse = lax.rsqrt(squares[...] / D + EPSILON)
        inverse = jnp.transpose(jnp.broadcast_to(inverse, (HEAD_DIM, inverse.shape[1])))

        def head(index):
            return total[:, index * HEAD_DIM : (index + 1) * HEAD_DIM] * inverse

        def turned(rows, gain):
            mean_square = jnp.mean(rows * rows, axis=-1, keepdims=True)
            rows = rows * lax.rsqrt(mean_square + EPSILON) * gain
            return rows * cos_ref[...] + pltpu.roll(rows, HEAD_DIM // 2, 1) * sin_ref[...]

        for index in range(2):
            query_ref[:, index * HEAD_DIM : (index + 1) * HEAD_DIM] = (
                turned(head(index), query_gain_ref[...]) * QUERY_SCALE
            ).astype(jnp.bfloat16)
        pair_ref[:, :HEAD_DIM] = turned(head(2), key_gain_ref[...]).astype(jnp.bfloat16)
        pair_ref[:, HEAD_DIM:] = head(3).astype(jnp.bfloat16)


def own_block(step, core):
    return step // 2 * 4 + core[0] * 2 + step % 2


def other_block(step, core):
    return step // 2 * 4 + (1 - core[0]) * 2 + step % 2


def qkv_specs(block_of, width, rows):
    def parts(height):
        return pl.BlockSpec((1, height, rows), lambda step, core: (block_of(step, core), 0, 0))

    return [
        parts(UPPER),
        parts(width - UPPER),
        pl.BlockSpec((1, width, 1), lambda step, core: (block_of(step, core), 0, 0)),
        pl.BlockSpec((8, 1, PAD_IN, 512), lambda step, core: (step % 2, step // 2, 0, 0)),
    ]


def project_first(core, upper, lower, gain, weights):
    count, _, rows = upper.shape
    width = WIDTH
    fixed = lambda step, core: (0, 0)
    return pl.pallas_call(
        first_kernel,
        grid_spec=pltpu.PrefetchScalarGridSpec(
            num_scalar_prefetch=1,
            grid=(count // 2,),
            in_specs=qkv_specs(own_block, width, rows),
            out_specs=[pl.BlockSpec((rows, 512), fixed), pl.BlockSpec((1, rows), fixed)],
            scratch_shapes=[pltpu.VMEM((width, 512), jnp.bfloat16)],
        ),
        out_shape=[
            jax.ShapeDtypeStruct((rows, 512), jnp.float32),
            jax.ShapeDtypeStruct((1, rows), jnp.float32),
        ],
        compiler_params=pltpu.CompilerParams(vmem_limit_bytes=VMEM),
        cost_estimate=pl.CostEstimate(
            flops=rows * 512 * D, bytes_accessed=5 * 2**20, transcendentals=0
        ),
    )(core, upper, lower, gain, weights)


def project_second(
    core, upper, lower, gain, weights, total, squares, cosine, sine, query_gain, key_gain
):
    count, _, rows = upper.shape
    width = WIDTH
    fixed = lambda step, core: (0, 0)
    return pl.pallas_call(
        second_kernel,
        grid_spec=pltpu.PrefetchScalarGridSpec(
            num_scalar_prefetch=1,
            grid=(count // 2,),
            in_specs=qkv_specs(other_block, width, rows)
            + [
                pl.BlockSpec((rows, 512), fixed),
                pl.BlockSpec((1, rows), fixed),
                pl.BlockSpec((rows, HEAD_DIM), fixed),
                pl.BlockSpec((rows, HEAD_DIM), fixed),
                pl.BlockSpec((1, HEAD_DIM), fixed),
                pl.BlockSpec((1, HEAD_DIM), fixed),
            ],
            out_specs=[pl.BlockSpec((rows, 256), fixed), pl.BlockSpec((rows, 256), fixed)],
            scratch_shapes=[
                pltpu.VMEM((width, 512), jnp.bfloat16),
                pltpu.VMEM((rows, 512), jnp.float32),
                pltpu.VMEM((1, rows), jnp.float32),
            ],
        ),
        out_shape=[
            jax.ShapeDtypeStruct((rows, 256), jnp.bfloat16),
            jax.ShapeDtypeStruct((rows, 256), jnp.bfloat16),
        ],
        compiler_params=pltpu.CompilerParams(vmem_limit_bytes=VMEM),
        cost_estimate=pl.CostEstimate(
            flops=rows * 512 * D, bytes_accessed=5 * 2**20, transcendentals=0
        ),
    )(
        core, upper, lower, gain, weights, total, squares, cosine, sine,
        query_gain[None, :], key_gain[None, :],
    )


def out_kernel(
    core_ref, own_ref, other_ref, along_ref, across_ref, result_ref, squares_ref, total
):
    step = pl.program_id(0)

    @pl.when(step == 0)
    def _():
        total[...] = jnp.zeros_like(total)

    for heads_ref, weight_ref in ((own_ref, along_ref), (other_ref, across_ref)):
        left = weight_ref[:, 0, :ROWS_OUT, :].reshape(8 * ROWS_OUT, 512)
        right = weight_ref[:, 0, ROWS_OUT:, :]
        right = jnp.concatenate([right[:, :, :256], right[:, :, 256:]], axis=1)
        right = right.reshape(8 * ROWS_OUT, 256)
        heads = heads_ref[0]
        for first, part in ((0, left), (512, right)):
            total[first : first + part.shape[1], :] += lax.dot_general(
                part, heads, (((0,), (0,)), ((), ())), preferred_element_type=jnp.float32
            )

    @pl.when(step == pl.num_programs(0) - 1)
    def _():
        result = total[:WIDTH, :]
        result_ref[...] = result
        squares_ref[...] = jnp.sum(result * result, axis=0, keepdims=True)


def project_out(core, heads, along, across):
    count, depth, rows = heads.shape
    fixed = lambda step, core: (0, 0)
    weights = pl.BlockSpec(
        (8, 1, PAD_ALL - PAD_IN, 512), lambda step, core: (step % 2, step // 2, 2, 0)
    )
    return pl.pallas_call(
        out_kernel,
        grid_spec=pltpu.PrefetchScalarGridSpec(
            num_scalar_prefetch=1,
            grid=(count // 2,),
            in_specs=[
                pl.BlockSpec((1, depth, rows), lambda step, core: (own_block(step, core), 0, 0)),
                pl.BlockSpec((1, depth, rows), lambda step, core: (other_block(step, core), 0, 0)),
                weights,
                weights,
            ],
            out_specs=[pl.BlockSpec((WIDTH, rows), fixed), pl.BlockSpec((1, rows), fixed)],
            scratch_shapes=[pltpu.VMEM((768, rows), jnp.float32)],
        ),
        out_shape=[
            jax.ShapeDtypeStruct((WIDTH, rows), jnp.float32),
            jax.ShapeDtypeStruct((1, rows), jnp.float32),
        ],
        compiler_params=pltpu.CompilerParams(vmem_limit_bytes=VMEM),
        cost_estimate=pl.CostEstimate(
            flops=2 * rows * 768 * 2048, bytes_accessed=5 * 2**20, transcendentals=0
        ),
    )(core, heads, heads, along, across)


def body(
    tokens,
    features,
    starts,
    sources,
    soft_gain,
    proj_weight,
    input_gain,
    query_weight,
    key_weight,
    value_weight,
    query_gain,
    key_gain,
    out_weight,
    post_gain,
):
    tok_rows, width = tokens.shape
    head_count = 8
    x_count = 4
    seq_count = x_count * Z
    core_index = lax.axis_index("core")
    z_index = lax.axis_index("z")
    seq_index = lax.axis_index(SEQ)
    total_rows = seq_count * tok_rows

    out_right = jnp.pad(out_weight[:, 512:], ((0, 0), (0, 768 - width)))
    local = jnp.concatenate(
        [
            jnp.pad(
                jnp.concatenate([query_weight, key_weight, value_weight], axis=1),
                ((0, PAD_IN - ROWS_IN), (0, 0)),
            ),
            out_weight[:, :512],
            jnp.concatenate([out_right[:16], out_right[16:]], axis=1),
        ],
        axis=0,
    )
    same_half = from_half(local, 0)
    other_half = from_half(local, 1)
    core = core_index.astype(jnp.int32)[None]

    image_count = starts.shape[0]
    vis = features.shape[2]
    pooled_side = PATCH_SIDE // POOL
    pool_rows = features.shape[0] // POOL
    block_rows = pool_rows * pooled_side
    shards_each = pooled_side // pool_rows
    patch_grid = features.reshape(pool_rows, POOL, pooled_side, POOL, vis)
    pooled = jnp.sum(patch_grid, axis=(1, 3), dtype=jnp.float32).reshape(block_rows, vis) / (
        POOL * POOL
    )
    soft = rms_scale(pooled, soft_gain).astype(jnp.bfloat16)
    vis_part = vis // 4
    soft, same_half, other_half = lax.optimization_barrier((soft, same_half, other_half))
    k_first = lax.axis_index("k") == 0
    both = jnp.stack(
        [
            jnp.where(k_first, same_half, other_half),
            jnp.where(k_first, other_half, same_half),
        ]
    )
    along = lax.all_gather(both, "z", axis=0)
    soft_part = lax.dynamic_slice_in_dim(soft, lax.axis_index("y") * vis_part, vis_part, 1)
    soft_z = exchange(soft_part, "z", Z).reshape(Z * block_rows, vis_part)
    soft_z, proj_weight, tokens = lax.optimization_barrier((soft_z, proj_weight, tokens))
    target = jnp.arange(x_count, dtype=jnp.int32)
    target_seq = (target // 2 * 2 + core_index) * Z + z_index
    frame_pos = (
        target_seq[:, None] * tok_rows + jnp.arange(tok_rows, dtype=jnp.int32)[None, :]
    ).reshape(-1)
    frame_image = image_of(frame_pos, starts)
    row_base = sources // shards_each * (block_rows * shards_each) - starts
    image_ids = jnp.arange(image_count, dtype=jnp.int32)
    frame_row = jnp.sum(
        jnp.where(frame_image[:, None] == image_ids[None, :], row_base[None, :], 0), axis=1
    )
    frame_row = jnp.where(frame_image >= 0, frame_row + frame_pos, -1)
    x_index = lax.axis_index(("k", "a"))
    here = x_index * (Z * block_rows) + jnp.arange(Z * block_rows, dtype=jnp.int32)
    chosen = (frame_row[:, None] == here[None, :]).astype(jnp.bfloat16)
    chosen = chosen.reshape(x_count, tok_rows, Z * block_rows)
    frames = jnp.einsum("sk,xps->xkp", soft_z, chosen, preferred_element_type=jnp.float32)
    frames = lax.all_to_all(frames.astype(jnp.bfloat16), ("k", "a"), 0, 0, tiled=True)
    mine = jnp.sum(frames.astype(jnp.float32), axis=0).astype(jnp.bfloat16)
    soft_rows = exchange(mine, "y", 4).reshape(vis, tok_rows)
    embedded = lax.dot_general(
        swapped(proj_weight), soft_rows, (((0,), (0,)), ((), ())),
        preferred_element_type=jnp.float32,
    ).astype(jnp.bfloat16)
    my_pos = seq_index * tok_rows + jnp.arange(tok_rows, dtype=jnp.int32)
    my_image = image_of(my_pos, starts)
    residual = jnp.where((my_image >= 0)[None, :], embedded, swapped(tokens).T)

    upper = exchange(residual[:UPPER], HEAD, head_count)
    lower = exchange(residual[UPPER:], HEAD, head_count)
    along, upper = lax.optimization_barrier((along, upper))
    across = lax.ppermute(along, "core", [(0, 1), (1, 0)])
    half = HEAD_DIM // 2
    frequency = ROPE_BASE ** (-jnp.arange(half, dtype=jnp.float32) * 2.0 / HEAD_DIM)
    angles = my_pos.astype(jnp.float32)[:, None] * frequency[None, :]
    cosine, sine = jnp.cos(angles), jnp.sin(angles)
    gain_parts = input_gain.reshape(head_count, width, 1)
    total, row_squares = project_first(core, upper, lower, gain_parts, along)
    queries, own = project_second(
        core,
        upper,
        lower,
        gain_parts,
        across,
        total,
        row_squares,
        jnp.concatenate([cosine, cosine], axis=1),
        jnp.concatenate([-sine, sine], axis=1),
        query_gain,
        key_gain,
    )
    past_count = WINDOW // tok_rows
    own, residual = lax.optimization_barrier((own, residual))
    given_residual = swapped(residual)
    near = jnp.concatenate([shifted(own, 2), shifted(own, 1)], axis=0)
    window = jnp.concatenate([shifted(near, 2), near, own, shifted(own, -1)], axis=0)
    window, given_residual = lax.optimization_barrier((window, given_residual))
    key_pos = (seq_index - past_count) * tok_rows + jnp.arange(window.shape[0], dtype=jnp.int32)
    allowed = allowed_keys(my_pos, key_pos, starts, total_rows)
    attended = attend(
        queries.reshape(tok_rows, 1, 2, HEAD_DIM),
        window[:, :HEAD_DIM].reshape(-1, 1, HEAD_DIM),
        window[:, HEAD_DIM:].reshape(-1, 1, HEAD_DIM),
        allowed,
    )
    attended = attended.reshape(tok_rows, 2 * HEAD_DIM).T
    heads_all = exchange(attended, HEAD, head_count)
    projected, squares = project_out(core, heads_all, along, across)
    given = swapped(projected.astype(jnp.bfloat16)).astype(jnp.float32)
    all_squares = exchange(squares, ("a", "y", "core"), 16).reshape(8, 2, tok_rows)
    from_core = jnp.arange(2, dtype=jnp.int32) == lax.axis_index("a")
    squares = jnp.sum(jnp.where(from_core[None, :, None], all_squares, 0.0), axis=(0, 1))
    post = given * lax.rsqrt(squares[None, :] / D + EPSILON) * post_gain[:, None]
    return (given_residual.astype(jnp.float32) + post).astype(jnp.bfloat16).T


def solution(mesh):
    split = Mesh(mesh.devices.reshape(2, 2, Z, 4, 2), ("k", "a", "z", "y", "core"))
    seq, head = GIVEN_SEQ, GIVEN_HEAD
    return jax.shard_map(
        body,
        mesh=split,
        in_specs=(
            P(seq, head),
            P(seq, None, None),
            P(),
            P(),
            P(),
            P(None, head),
            P(),
            P(seq, head),
            P(seq, head),
            P(seq, head),
            P(),
            P(),
            P(seq, head),
            P(head),
        ),
        out_specs=P(seq, head),
        check_vma=False,
    )
```

```python
import jax
import jax.numpy as jnp
from jax import lax
from jax.experimental import pallas as pl
from jax.experimental.pallas import tpu as pltpu
from jax.sharding import Mesh
from jax.sharding import PartitionSpec as P

D = 5376
HEAD_DIM = 128
WINDOW = 1024
PATCH_SIDE = 64
POOL = 4
IMG_TOK = 256
Z = 16
ROWS_IN = 84
ROWS_OUT = 32
PAD_IN = 96
PAD_ALL = 144
WIDTH = 672

EPSILON = 1e-06
QUERY_SCALE = 168.0 ** (-0.5)
ROPE_BASE = 10000.0

GIVEN_SEQ = ("k", "a", "z")
GIVEN_HEAD = ("y", "core")
SEQ = ("k", "core", "z")
HEAD = ("y", "a")


def swapped(value):
    return lax.ppermute(value, ("a", "core"), [(0, 0), (1, 2), (2, 1), (3, 3)])


def from_half(value, flip):
    pairs = []
    for k in range(2):
        for a in range(2):
            for core in range(2):
                pairs.append(((k * 2 + a) * 2 + core, ((k ^ flip) * 2 + core) * 2 + a))
    return lax.ppermute(value, ("k", "a", "core"), pairs)


def shifted(value, steps):
    pairs = []
    for source in range(4 * Z):
        target = source + steps
        if 0 <= target < 4 * Z:
            place = [
                ((shard // (2 * Z)) * Z + shard % Z) * 2 + shard // Z % 2
                for shard in (source, target)
            ]
            pairs.append((place[0], place[1]))
    return lax.ppermute(value, ("k", "z", "core"), pairs)


def exchange(value, axes, count):
    spread = jnp.broadcast_to(value[None], (count, *value.shape))
    return lax.all_to_all(spread, axes, 0, 0, tiled=True)


def rms_scale(inputs, scale_gain):
    return (
        inputs * lax.rsqrt(jnp.mean(inputs * inputs, axis=-1, keepdims=True) + EPSILON) * scale_gain
    )


def image_of(positions, starts):
    inside = (positions[:, None] >= starts[None, :]) & (
        positions[:, None] < starts[None, :] + IMG_TOK
    )
    labels = jnp.arange(1, starts.shape[0] + 1, dtype=jnp.int32)
    return jnp.sum(jnp.where(inside, labels[None, :], 0), axis=1) - 1


def allowed_keys(query_pos, key_pos, starts, total_rows):
    query_img = image_of(query_pos, starts)
    key_img = image_of(key_pos, starts)
    inside = (key_pos >= 0) & (key_pos < total_rows)
    in_window = query_pos[:, None] - key_pos[None, :] < WINDOW
    causal = key_pos[None, :] <= query_pos[:, None]
    same_image = (query_img[:, None] == key_img[None, :]) & (query_img[:, None] >= 0)
    return inside[None, :] & in_window & (causal | same_image)


def attend(queries, key_rows, values, allowed):
    scores = jnp.einsum("qgrd,kgd->grqk", queries, key_rows, preferred_element_type=jnp.float32)
    scores = jnp.where(allowed[None, None], scores, -jnp.inf)
    row_max = jnp.max(scores, axis=-1, keepdims=True)
    weights = jnp.exp(scores - row_max)
    row_sum = jnp.sum(weights, axis=-1)
    mixed_heads = jnp.einsum(
        "grqk,kgd->qgrd", weights.astype(jnp.bfloat16), values, preferred_element_type=jnp.float32
    )
    return (mixed_heads / jnp.transpose(row_sum, (2, 0, 1))[..., None]).astype(jnp.bfloat16)


def add_part(whole_ref, gain_ref, weight_ref, block, start, squares):
    for shard in range(8):
        block[shard * ROWS_IN : (shard + 1) * ROWS_IN, :] = weight_ref[shard, 0, :ROWS_IN, :]
    part = whole_ref[0].astype(jnp.float32)
    scaled = (part * gain_ref[0]).astype(jnp.bfloat16)
    product = lax.dot_general(
        scaled, block[...], (((0,), (0,)), ((), ())), preferred_element_type=jnp.float32
    )
    return start + product, squares + jnp.sum(part * part, axis=0, keepdims=True)


def first_kernel(core_ref, whole_ref, gain_ref, weight_ref, total_ref, squares_ref, block):
    @pl.when(pl.program_id(0) == 0)
    def _():
        total_ref[...] = jnp.zeros_like(total_ref)
        squares_ref[...] = jnp.zeros_like(squares_ref)

    total_ref[...], squares_ref[...] = add_part(
        whole_ref, gain_ref, weight_ref, block, total_ref[...], squares_ref[...]
    )


def second_kernel(
    core_ref, whole_ref, gain_ref, weight_ref, start_ref, square_ref, cos_ref, sin_ref,
    query_gain_ref, key_gain_ref, query_ref, pair_ref, block, total, squares,
):
    step = pl.program_id(0)

    @pl.when(step == 0)
    def _():
        total[...] = start_ref[...]
        squares[...] = square_ref[...]

    total[...], squares[...] = add_part(
        whole_ref, gain_ref, weight_ref, block, total[...], squares[...]
    )

    @pl.when(step == pl.num_programs(0) - 1)
    def _():
        inverse = lax.rsqrt(squares[...] / D + EPSILON)
        inverse = jnp.transpose(jnp.broadcast_to(inverse, (HEAD_DIM, inverse.shape[1])))

        def head(index):
            return total[:, index * HEAD_DIM : (index + 1) * HEAD_DIM] * inverse

        def turned(rows, gain):
            mean_square = jnp.mean(rows * rows, axis=-1, keepdims=True)
            rows = rows * lax.rsqrt(mean_square + EPSILON) * gain
            return rows * cos_ref[...] + pltpu.roll(rows, HEAD_DIM // 2, 1) * sin_ref[...]

        for index in range(2):
            query_ref[:, index * HEAD_DIM : (index + 1) * HEAD_DIM] = (
                turned(head(index), query_gain_ref[...]) * QUERY_SCALE
            ).astype(jnp.bfloat16)
        pair_ref[:, :HEAD_DIM] = turned(head(2), key_gain_ref[...]).astype(jnp.bfloat16)
        pair_ref[:, HEAD_DIM:] = head(3).astype(jnp.bfloat16)


def own_block(step, core):
    return step // 2 * 4 + core[0] * 2 + step % 2


def other_block(step, core):
    return step // 2 * 4 + (1 - core[0]) * 2 + step % 2


def qkv_specs(block_of, width, rows):
    return [
        pl.BlockSpec((1, width, rows), lambda step, core: (block_of(step, core), 0, 0)),
        pl.BlockSpec((1, width, 1), lambda step, core: (block_of(step, core), 0, 0)),
        pl.BlockSpec((8, 1, PAD_IN, 512), lambda step, core: (step % 2, step // 2, 0, 0)),
    ]


def project_first(core, whole, gain, weights):
    count, width, rows = whole.shape
    fixed = lambda step, core: (0, 0)
    return pl.pallas_call(
        first_kernel,
        grid_spec=pltpu.PrefetchScalarGridSpec(
            num_scalar_prefetch=1,
            grid=(count // 2,),
            in_specs=qkv_specs(own_block, width, rows),
            out_specs=[pl.BlockSpec((rows, 512), fixed), pl.BlockSpec((1, rows), fixed)],
            scratch_shapes=[pltpu.VMEM((width, 512), jnp.bfloat16)],
        ),
        out_shape=[
            jax.ShapeDtypeStruct((rows, 512), jnp.float32),
            jax.ShapeDtypeStruct((1, rows), jnp.float32),
        ],
        compiler_params=pltpu.CompilerParams(vmem_limit_bytes=24 * 2**20),
        cost_estimate=pl.CostEstimate(
            flops=rows * 512 * D, bytes_accessed=5 * 2**20, transcendentals=0
        ),
    )(core, whole, gain, weights)


def project_second(
    core, whole, gain, weights, total, squares, cosine, sine, query_gain, key_gain
):
    count, width, rows = whole.shape
    fixed = lambda step, core: (0, 0)
    return pl.pallas_call(
        second_kernel,
        grid_spec=pltpu.PrefetchScalarGridSpec(
            num_scalar_prefetch=1,
            grid=(count // 2,),
            in_specs=qkv_specs(other_block, width, rows)
            + [
                pl.BlockSpec((rows, 512), fixed),
                pl.BlockSpec((1, rows), fixed),
                pl.BlockSpec((rows, HEAD_DIM), fixed),
                pl.BlockSpec((rows, HEAD_DIM), fixed),
                pl.BlockSpec((1, HEAD_DIM), fixed),
                pl.BlockSpec((1, HEAD_DIM), fixed),
            ],
            out_specs=[pl.BlockSpec((rows, 256), fixed), pl.BlockSpec((rows, 256), fixed)],
            scratch_shapes=[
                pltpu.VMEM((width, 512), jnp.bfloat16),
                pltpu.VMEM((rows, 512), jnp.float32),
                pltpu.VMEM((1, rows), jnp.float32),
            ],
        ),
        out_shape=[
            jax.ShapeDtypeStruct((rows, 256), jnp.bfloat16),
            jax.ShapeDtypeStruct((rows, 256), jnp.bfloat16),
        ],
        compiler_params=pltpu.CompilerParams(vmem_limit_bytes=24 * 2**20),
        cost_estimate=pl.CostEstimate(
            flops=rows * 512 * D, bytes_accessed=5 * 2**20, transcendentals=0
        ),
    )(
        core, whole, gain, weights, total, squares, cosine, sine,
        query_gain[None, :], key_gain[None, :],
    )


def out_kernel(
    core_ref, own_ref, other_ref, along_ref, across_ref, result_ref, squares_ref, total
):
    step = pl.program_id(0)

    @pl.when(step == 0)
    def _():
        total[...] = jnp.zeros_like(total)

    for heads_ref, weight_ref in ((own_ref, along_ref), (other_ref, across_ref)):
        left = weight_ref[:, 0, :ROWS_OUT, :].reshape(8 * ROWS_OUT, 512)
        right = weight_ref[:, 0, ROWS_OUT:, :]
        right = jnp.concatenate([right[:, :, :256], right[:, :, 256:]], axis=1)
        right = right.reshape(8 * ROWS_OUT, 256)
        heads = heads_ref[0]
        for first, part in ((0, left), (512, right)):
            total[first : first + part.shape[1], :] += lax.dot_general(
                part, heads, (((0,), (0,)), ((), ())), preferred_element_type=jnp.float32
            )

    @pl.when(step == pl.num_programs(0) - 1)
    def _():
        result = total[:WIDTH, :]
        result_ref[...] = result
        squares_ref[...] = jnp.sum(result * result, axis=0, keepdims=True)


def project_out(core, heads, along, across):
    count, depth, rows = heads.shape
    fixed = lambda step, core: (0, 0)
    weights = pl.BlockSpec(
        (8, 1, PAD_ALL - PAD_IN, 512), lambda step, core: (step % 2, step // 2, 2, 0)
    )
    return pl.pallas_call(
        out_kernel,
        grid_spec=pltpu.PrefetchScalarGridSpec(
            num_scalar_prefetch=1,
            grid=(count // 2,),
            in_specs=[
                pl.BlockSpec((1, depth, rows), lambda step, core: (own_block(step, core), 0, 0)),
                pl.BlockSpec((1, depth, rows), lambda step, core: (other_block(step, core), 0, 0)),
                weights,
                weights,
            ],
            out_specs=[pl.BlockSpec((WIDTH, rows), fixed), pl.BlockSpec((1, rows), fixed)],
            scratch_shapes=[pltpu.VMEM((768, rows), jnp.float32)],
        ),
        out_shape=[
            jax.ShapeDtypeStruct((WIDTH, rows), jnp.float32),
            jax.ShapeDtypeStruct((1, rows), jnp.float32),
        ],
        compiler_params=pltpu.CompilerParams(vmem_limit_bytes=24 * 2**20),
        cost_estimate=pl.CostEstimate(
            flops=2 * rows * 768 * 2048, bytes_accessed=5 * 2**20, transcendentals=0
        ),
    )(core, heads, heads, along, across)


def body(
    tokens,
    features,
    starts,
    sources,
    soft_gain,
    proj_weight,
    input_gain,
    query_weight,
    key_weight,
    value_weight,
    query_gain,
    key_gain,
    out_weight,
    post_gain,
):
    tok_rows, width = tokens.shape
    head_count = 8
    x_count = 4
    seq_count = x_count * Z
    core_index = lax.axis_index("core")
    z_index = lax.axis_index("z")
    seq_index = lax.axis_index(SEQ)
    total_rows = seq_count * tok_rows

    out_right = jnp.pad(out_weight[:, 512:], ((0, 0), (0, 768 - width)))
    local = jnp.concatenate(
        [
            jnp.pad(
                jnp.concatenate([query_weight, key_weight, value_weight], axis=1),
                ((0, PAD_IN - ROWS_IN), (0, 0)),
            ),
            out_weight[:, :512],
            jnp.concatenate([out_right[:16], out_right[16:]], axis=1),
        ],
        axis=0,
    )
    same_half = from_half(local, 0)
    other_half = from_half(local, 1)
    k_first = lax.axis_index("k") == 0
    both = jnp.stack(
        [
            jnp.where(k_first, same_half, other_half),
            jnp.where(k_first, other_half, same_half),
        ]
    )
    core = core_index.astype(jnp.int32)[None]

    image_count = starts.shape[0]
    vis = features.shape[2]
    pooled_side = PATCH_SIDE // POOL
    pool_rows = features.shape[0] // POOL
    block_rows = pool_rows * pooled_side
    shards_each = pooled_side // pool_rows
    patch_grid = features.reshape(pool_rows, POOL, pooled_side, POOL, vis)
    pooled = jnp.sum(patch_grid, axis=(1, 3), dtype=jnp.float32).reshape(block_rows, vis) / (
        POOL * POOL
    )
    soft = rms_scale(pooled, soft_gain).astype(jnp.bfloat16)
    vis_part = vis // head_count
    soft_part = lax.dynamic_slice_in_dim(
        soft, lax.axis_index(GIVEN_HEAD) * vis_part, vis_part, 1
    )
    soft_z = exchange(soft_part, "z", Z).reshape(Z * block_rows, vis_part)
    soft_z, both = lax.optimization_barrier((soft_z, both))
    along = lax.all_gather(both, "z", axis=0)
    proj_weight, tokens = swapped(proj_weight), swapped(tokens)
    soft_z, proj_weight, tokens = lax.optimization_barrier((soft_z, proj_weight, tokens))
    target = jnp.arange(8, dtype=jnp.int32)
    target_k, target_a, target_core = target // 4, target // 2 % 2, target % 2
    target_seq = (target_k * 2 + target_core) * Z + z_index
    frame_pos = (
        target_seq[:, None] * tok_rows + jnp.arange(tok_rows, dtype=jnp.int32)[None, :]
    ).reshape(-1)
    frame_image = image_of(frame_pos, starts)
    row_base = sources // shards_each * (block_rows * shards_each) - starts
    image_ids = jnp.arange(image_count, dtype=jnp.int32)
    frame_row = jnp.sum(
        jnp.where(frame_image[:, None] == image_ids[None, :], row_base[None, :], 0), axis=1
    )
    wanted = (frame_image >= 0) & jnp.repeat(target_a == core_index, tok_rows)
    frame_row = jnp.where(wanted, frame_row + frame_pos, -1)
    x_index = lax.axis_index(("k", "a"))
    here = x_index * (Z * block_rows) + jnp.arange(Z * block_rows, dtype=jnp.int32)
    chosen = (frame_row[:, None] == here[None, :]).astype(jnp.bfloat16)
    chosen = chosen.reshape(8, tok_rows, Z * block_rows)
    frames = jnp.einsum("sk,xps->xkp", soft_z, chosen, preferred_element_type=jnp.float32)
    frames = lax.all_to_all(
        frames.astype(jnp.bfloat16), ("k", "a", "core"), 0, 0, tiled=True
    )
    mine = jnp.sum(frames.astype(jnp.float32), axis=0).astype(jnp.bfloat16)
    soft_rows = exchange(mine, HEAD, head_count).reshape(vis, tok_rows)
    embedded = lax.dot_general(
        proj_weight, soft_rows, (((0,), (0,)), ((), ())),
        preferred_element_type=jnp.float32,
    ).astype(jnp.bfloat16)
    my_pos = seq_index * tok_rows + jnp.arange(tok_rows, dtype=jnp.int32)
    my_image = image_of(my_pos, starts)
    residual = jnp.where((my_image >= 0)[None, :], embedded, tokens.T)

    whole = exchange(residual, HEAD, head_count)
    given_residual = swapped(residual)
    along, whole, given_residual = lax.optimization_barrier((along, whole, given_residual))
    across = lax.ppermute(along, "core", [(0, 1), (1, 0)])
    half = HEAD_DIM // 2
    frequency = ROPE_BASE ** (-jnp.arange(half, dtype=jnp.float32) * 2.0 / HEAD_DIM)
    angles = my_pos.astype(jnp.float32)[:, None] * frequency[None, :]
    cosine, sine = jnp.cos(angles), jnp.sin(angles)
    gain_parts = input_gain.reshape(head_count, width, 1)
    total, row_squares = project_first(core, whole, gain_parts, along)
    queries, own = project_second(
        core,
        whole,
        gain_parts,
        across,
        total,
        row_squares,
        jnp.concatenate([cosine, cosine], axis=1),
        jnp.concatenate([-sine, sine], axis=1),
        query_gain,
        key_gain,
    )
    past_count = WINDOW // tok_rows
    near = jnp.concatenate([shifted(own, 2), shifted(own, 1)], axis=0)
    window = jnp.concatenate([shifted(near, 2), near, own, shifted(own, -1)], axis=0)
    key_pos = (seq_index - past_count) * tok_rows + jnp.arange(window.shape[0], dtype=jnp.int32)
    allowed = allowed_keys(my_pos, key_pos, starts, total_rows)
    attended = attend(
        queries.reshape(tok_rows, 1, 2, HEAD_DIM),
        window[:, :HEAD_DIM].reshape(-1, 1, HEAD_DIM),
        window[:, HEAD_DIM:].reshape(-1, 1, HEAD_DIM),
        allowed,
    )
    attended = attended.reshape(tok_rows, 2 * HEAD_DIM).T
    heads_all = exchange(attended, HEAD, head_count)
    projected, squares = project_out(core, heads_all, along, across)
    given = swapped(projected.astype(jnp.bfloat16)).astype(jnp.float32)
    all_squares = exchange(squares, ("a", "y", "core"), 16).reshape(8, 2, tok_rows)
    from_core = jnp.arange(2, dtype=jnp.int32) == lax.axis_index("a")
    squares = jnp.sum(jnp.where(from_core[None, :, None], all_squares, 0.0), axis=(0, 1))
    post = given * lax.rsqrt(squares[None, :] / D + EPSILON) * post_gain[:, None]
    return (given_residual.astype(jnp.float32) + post).astype(jnp.bfloat16).T


def solution(mesh):
    split = Mesh(mesh.devices.reshape(2, 2, Z, 4, 2), ("k", "a", "z", "y", "core"))
    seq, head = GIVEN_SEQ, GIVEN_HEAD
    return jax.shard_map(
        body,
        mesh=split,
        in_specs=(
            P(seq, head),
            P(seq, None, None),
            P(),
            P(),
            P(),
            P(None, head),
            P(),
            P(seq, head),
            P(seq, head),
            P(seq, head),
            P(),
            P(),
            P(seq, head),
            P(head),
        ),
        out_specs=P(seq, head),
        check_vma=False,
    )
```

```python
import jax
import jax.numpy as jnp
from jax import lax
from jax.experimental import pallas as pl
from jax.experimental.pallas import tpu as pltpu
from jax.sharding import Mesh
from jax.sharding import PartitionSpec as P

D = 5376
HEAD_DIM = 128
WINDOW = 1024
PATCH_SIDE = 64
POOL = 4
IMG_TOK = 256
Z = 16
ROWS_IN = 84
ROWS_OUT = 32
PAD_IN = 96
PAD_ALL = 144
WIDTH = 672

EPSILON = 1e-06
QUERY_SCALE = 168.0 ** (-0.5)
ROPE_BASE = 10000.0

GIVEN_SEQ = ("k", "a", "z")
GIVEN_HEAD = ("y", "core")
SEQ = ("k", "core", "z")
HEAD = ("y", "a")


def swapped(value):
    return lax.ppermute(value, ("a", "core"), [(0, 0), (1, 2), (2, 1), (3, 3)])


def from_half(value, flip):
    pairs = []
    for k in range(2):
        for a in range(2):
            for core in range(2):
                pairs.append(((k * 2 + a) * 2 + core, ((k ^ flip) * 2 + core) * 2 + a))
    return lax.ppermute(value, ("k", "a", "core"), pairs)


def shifted(value, steps):
    pairs = []
    for source in range(4 * Z):
        target = source + steps
        if 0 <= target < 4 * Z:
            place = [
                ((shard // (2 * Z)) * Z + shard % Z) * 2 + shard // Z % 2
                for shard in (source, target)
            ]
            pairs.append((place[0], place[1]))
    return lax.ppermute(value, ("k", "z", "core"), pairs)


def exchange(value, axes, count):
    spread = jnp.broadcast_to(value[None], (count, *value.shape))
    return lax.all_to_all(spread, axes, 0, 0, tiled=True)


def rms_scale(inputs, scale_gain):
    return (
        inputs * lax.rsqrt(jnp.mean(inputs * inputs, axis=-1, keepdims=True) + EPSILON) * scale_gain
    )


def image_of(positions, starts):
    inside = (positions[:, None] >= starts[None, :]) & (
        positions[:, None] < starts[None, :] + IMG_TOK
    )
    labels = jnp.arange(1, starts.shape[0] + 1, dtype=jnp.int32)
    return jnp.sum(jnp.where(inside, labels[None, :], 0), axis=1) - 1


def allowed_keys(query_pos, key_pos, starts, total_rows):
    query_img = image_of(query_pos, starts)
    key_img = image_of(key_pos, starts)
    inside = (key_pos >= 0) & (key_pos < total_rows)
    in_window = query_pos[:, None] - key_pos[None, :] < WINDOW
    causal = key_pos[None, :] <= query_pos[:, None]
    same_image = (query_img[:, None] == key_img[None, :]) & (query_img[:, None] >= 0)
    return inside[None, :] & in_window & (causal | same_image)


def attend(queries, key_rows, values, allowed):
    scores = jnp.einsum("qgrd,kgd->grqk", queries, key_rows, preferred_element_type=jnp.float32)
    scores = jnp.where(allowed[None, None], scores, -jnp.inf)
    row_max = jnp.max(scores, axis=-1, keepdims=True)
    weights = jnp.exp(scores - row_max)
    row_sum = jnp.sum(weights, axis=-1)
    mixed_heads = jnp.einsum(
        "grqk,kgd->qgrd", weights.astype(jnp.bfloat16), values, preferred_element_type=jnp.float32
    )
    return (mixed_heads / jnp.transpose(row_sum, (2, 0, 1))[..., None]).astype(jnp.bfloat16)


def add_part(whole_ref, gain_ref, weight_ref, block, start, squares):
    for shard in range(8):
        block[shard * ROWS_IN : (shard + 1) * ROWS_IN, :] = weight_ref[shard, 0, :ROWS_IN, :]
    part = whole_ref[0].astype(jnp.float32)
    scaled = (part * gain_ref[0]).astype(jnp.bfloat16)
    product = lax.dot_general(
        scaled, block[...], (((0,), (0,)), ((), ())), preferred_element_type=jnp.float32
    )
    return start + product, squares + jnp.sum(part * part, axis=0, keepdims=True)


def first_kernel(core_ref, whole_ref, gain_ref, weight_ref, total_ref, squares_ref, block):
    @pl.when(pl.program_id(0) == 0)
    def _():
        total_ref[...] = jnp.zeros_like(total_ref)
        squares_ref[...] = jnp.zeros_like(squares_ref)

    total_ref[...], squares_ref[...] = add_part(
        whole_ref, gain_ref, weight_ref, block, total_ref[...], squares_ref[...]
    )


def second_kernel(
    core_ref, whole_ref, gain_ref, weight_ref, start_ref, square_ref, cos_ref, sin_ref,
    query_gain_ref, key_gain_ref, query_ref, pair_ref, block, total, squares,
):
    step = pl.program_id(0)

    @pl.when(step == 0)
    def _():
        total[...] = start_ref[...]
        squares[...] = square_ref[...]

    total[...], squares[...] = add_part(
        whole_ref, gain_ref, weight_ref, block, total[...], squares[...]
    )

    @pl.when(step == pl.num_programs(0) - 1)
    def _():
        inverse = lax.rsqrt(squares[...] / D + EPSILON)
        inverse = jnp.transpose(jnp.broadcast_to(inverse, (HEAD_DIM, inverse.shape[1])))

        def head(index):
            return total[:, index * HEAD_DIM : (index + 1) * HEAD_DIM] * inverse

        def turned(rows, gain):
            mean_square = jnp.mean(rows * rows, axis=-1, keepdims=True)
            rows = rows * lax.rsqrt(mean_square + EPSILON) * gain
            return rows * cos_ref[...] + pltpu.roll(rows, HEAD_DIM // 2, 1) * sin_ref[...]

        for index in range(2):
            query_ref[:, index * HEAD_DIM : (index + 1) * HEAD_DIM] = (
                turned(head(index), query_gain_ref[...]) * QUERY_SCALE
            ).astype(jnp.bfloat16)
        pair_ref[:, :HEAD_DIM] = turned(head(2), key_gain_ref[...]).astype(jnp.bfloat16)
        pair_ref[:, HEAD_DIM:] = head(3).astype(jnp.bfloat16)


def own_block(step, core):
    return step // 2 * 4 + core[0] * 2 + step % 2


def other_block(step, core):
    return step // 2 * 4 + (1 - core[0]) * 2 + step % 2


def qkv_specs(block_of, width, rows):
    return [
        pl.BlockSpec((1, width, rows), lambda step, core: (block_of(step, core), 0, 0)),
        pl.BlockSpec((1, width, 1), lambda step, core: (block_of(step, core), 0, 0)),
        pl.BlockSpec((8, 1, PAD_IN, 512), lambda step, core: (step % 2, step // 2, 0, 0)),
    ]


def project_first(core, whole, gain, weights):
    count, width, rows = whole.shape
    fixed = lambda step, core: (0, 0)
    return pl.pallas_call(
        first_kernel,
        grid_spec=pltpu.PrefetchScalarGridSpec(
            num_scalar_prefetch=1,
            grid=(count // 2,),
            in_specs=qkv_specs(own_block, width, rows),
            out_specs=[pl.BlockSpec((rows, 512), fixed), pl.BlockSpec((1, rows), fixed)],
            scratch_shapes=[pltpu.VMEM((width, 512), jnp.bfloat16)],
        ),
        out_shape=[
            jax.ShapeDtypeStruct((rows, 512), jnp.float32),
            jax.ShapeDtypeStruct((1, rows), jnp.float32),
        ],
        compiler_params=pltpu.CompilerParams(vmem_limit_bytes=24 * 2**20),
        cost_estimate=pl.CostEstimate(
            flops=rows * 512 * D, bytes_accessed=5 * 2**20, transcendentals=0
        ),
    )(core, whole, gain, weights)


def project_second(
    core, whole, gain, weights, total, squares, cosine, sine, query_gain, key_gain
):
    count, width, rows = whole.shape
    fixed = lambda step, core: (0, 0)
    return pl.pallas_call(
        second_kernel,
        grid_spec=pltpu.PrefetchScalarGridSpec(
            num_scalar_prefetch=1,
            grid=(count // 2,),
            in_specs=qkv_specs(other_block, width, rows)
            + [
                pl.BlockSpec((rows, 512), fixed),
                pl.BlockSpec((1, rows), fixed),
                pl.BlockSpec((rows, HEAD_DIM), fixed),
                pl.BlockSpec((rows, HEAD_DIM), fixed),
                pl.BlockSpec((1, HEAD_DIM), fixed),
                pl.BlockSpec((1, HEAD_DIM), fixed),
            ],
            out_specs=[pl.BlockSpec((rows, 256), fixed), pl.BlockSpec((rows, 256), fixed)],
            scratch_shapes=[
                pltpu.VMEM((width, 512), jnp.bfloat16),
                pltpu.VMEM((rows, 512), jnp.float32),
                pltpu.VMEM((1, rows), jnp.float32),
            ],
        ),
        out_shape=[
            jax.ShapeDtypeStruct((rows, 256), jnp.bfloat16),
            jax.ShapeDtypeStruct((rows, 256), jnp.bfloat16),
        ],
        compiler_params=pltpu.CompilerParams(vmem_limit_bytes=24 * 2**20),
        cost_estimate=pl.CostEstimate(
            flops=rows * 512 * D, bytes_accessed=5 * 2**20, transcendentals=0
        ),
    )(
        core, whole, gain, weights, total, squares, cosine, sine,
        query_gain[None, :], key_gain[None, :],
    )


def out_kernel(
    core_ref, own_ref, other_ref, along_ref, across_ref, result_ref, squares_ref, total
):
    step = pl.program_id(0)

    @pl.when(step == 0)
    def _():
        total[...] = jnp.zeros_like(total)

    for heads_ref, weight_ref in ((own_ref, along_ref), (other_ref, across_ref)):
        left = weight_ref[:, 0, :ROWS_OUT, :].reshape(8 * ROWS_OUT, 512)
        right = weight_ref[:, 0, ROWS_OUT:, :]
        right = jnp.concatenate([right[:, :, :256], right[:, :, 256:]], axis=1)
        right = right.reshape(8 * ROWS_OUT, 256)
        heads = heads_ref[0]
        for first, part in ((0, left), (512, right)):
            total[first : first + part.shape[1], :] += lax.dot_general(
                part, heads, (((0,), (0,)), ((), ())), preferred_element_type=jnp.float32
            )

    @pl.when(step == pl.num_programs(0) - 1)
    def _():
        result = total[:WIDTH, :]
        result_ref[...] = result
        squares_ref[...] = jnp.sum(result * result, axis=0, keepdims=True)


def project_out(core, heads, along, across):
    count, depth, rows = heads.shape
    fixed = lambda step, core: (0, 0)
    weights = pl.BlockSpec(
        (8, 1, PAD_ALL - PAD_IN, 512), lambda step, core: (step % 2, step // 2, 2, 0)
    )
    return pl.pallas_call(
        out_kernel,
        grid_spec=pltpu.PrefetchScalarGridSpec(
            num_scalar_prefetch=1,
            grid=(count // 2,),
            in_specs=[
                pl.BlockSpec((1, depth, rows), lambda step, core: (own_block(step, core), 0, 0)),
                pl.BlockSpec((1, depth, rows), lambda step, core: (other_block(step, core), 0, 0)),
                weights,
                weights,
            ],
            out_specs=[pl.BlockSpec((WIDTH, rows), fixed), pl.BlockSpec((1, rows), fixed)],
            scratch_shapes=[pltpu.VMEM((768, rows), jnp.float32)],
        ),
        out_shape=[
            jax.ShapeDtypeStruct((WIDTH, rows), jnp.float32),
            jax.ShapeDtypeStruct((1, rows), jnp.float32),
        ],
        compiler_params=pltpu.CompilerParams(vmem_limit_bytes=24 * 2**20),
        cost_estimate=pl.CostEstimate(
            flops=2 * rows * 768 * 2048, bytes_accessed=5 * 2**20, transcendentals=0
        ),
    )(core, heads, heads, along, across)


def body(
    tokens,
    features,
    starts,
    sources,
    soft_gain,
    proj_weight,
    input_gain,
    query_weight,
    key_weight,
    value_weight,
    query_gain,
    key_gain,
    out_weight,
    post_gain,
):
    tok_rows, width = tokens.shape
    head_count = 8
    x_count = 4
    seq_count = x_count * Z
    core_index = lax.axis_index("core")
    z_index = lax.axis_index("z")
    seq_index = lax.axis_index(SEQ)
    total_rows = seq_count * tok_rows

    out_right = jnp.pad(out_weight[:, 512:], ((0, 0), (0, 768 - width)))
    local = jnp.concatenate(
        [
            jnp.pad(
                jnp.concatenate([query_weight, key_weight, value_weight], axis=1),
                ((0, PAD_IN - ROWS_IN), (0, 0)),
            ),
            out_weight[:, :512],
            jnp.concatenate([out_right[:16], out_right[16:]], axis=1),
        ],
        axis=0,
    )
    same_half = from_half(local, 0)
    other_half = from_half(local, 1)
    k_first = lax.axis_index("k") == 0
    both = jnp.stack(
        [
            jnp.where(k_first, same_half, other_half),
            jnp.where(k_first, other_half, same_half),
        ]
    )
    core = core_index.astype(jnp.int32)[None]

    image_count = starts.shape[0]
    vis = features.shape[2]
    pooled_side = PATCH_SIDE // POOL
    pool_rows = features.shape[0] // POOL
    block_rows = pool_rows * pooled_side
    shards_each = pooled_side // pool_rows
    row = jnp.arange(block_rows, dtype=jnp.int32)
    patch = jnp.arange(features.shape[0] * PATCH_SIDE, dtype=jnp.int32)
    square = patch // (PATCH_SIDE * POOL) * pooled_side + patch % PATCH_SIDE // POOL
    ones = (row[:, None] == square[None, :]).astype(jnp.bfloat16)
    pooled = jnp.dot(
        ones, features.reshape(-1, vis), preferred_element_type=jnp.float32
    ) / (POOL * POOL)
    soft = rms_scale(pooled, soft_gain).astype(jnp.bfloat16)
    vis_part = vis // head_count
    soft_part = lax.dynamic_slice_in_dim(
        soft, lax.axis_index(GIVEN_HEAD) * vis_part, vis_part, 1
    )
    soft_z = exchange(soft_part, "z", Z).reshape(Z * block_rows, vis_part)
    proj_other = lax.ppermute(proj_weight, ("a", "core"), [(0, 1), (3, 2)])
    tokens = swapped(tokens)
    soft_z, both, tokens, proj_other = lax.optimization_barrier(
        (soft_z, both, tokens, proj_other)
    )
    along = lax.all_gather(both, "z", axis=0)
    proj_weight = jnp.where(core_index == lax.axis_index("a"), proj_weight, proj_other)
    target = jnp.arange(8, dtype=jnp.int32)
    target_k, target_a, target_core = target // 4, target // 2 % 2, target % 2
    target_seq = (target_k * 2 + target_core) * Z + z_index
    frame_pos = (
        target_seq[:, None] * tok_rows + jnp.arange(tok_rows, dtype=jnp.int32)[None, :]
    ).reshape(-1)
    frame_image = image_of(frame_pos, starts)
    row_base = sources // shards_each * (block_rows * shards_each) - starts
    image_ids = jnp.arange(image_count, dtype=jnp.int32)
    frame_row = jnp.sum(
        jnp.where(frame_image[:, None] == image_ids[None, :], row_base[None, :], 0), axis=1
    )
    wanted = (frame_image >= 0) & jnp.repeat(target_a == core_index, tok_rows)
    frame_row = jnp.where(wanted, frame_row + frame_pos, -1)
    x_index = lax.axis_index(("k", "a"))
    here = x_index * (Z * block_rows) + jnp.arange(Z * block_rows, dtype=jnp.int32)
    chosen = (frame_row[:, None] == here[None, :]).astype(jnp.bfloat16)
    chosen = chosen.reshape(8, tok_rows, Z * block_rows)
    frames = jnp.einsum("sk,xps->xkp", soft_z, chosen, preferred_element_type=jnp.float32)
    frames = lax.all_to_all(
        frames.astype(jnp.bfloat16), ("k", "a", "core"), 0, 0, tiled=True
    )
    mine = jnp.sum(frames.astype(jnp.float32), axis=0).astype(jnp.bfloat16)
    soft_rows = exchange(mine, HEAD, head_count).reshape(vis, tok_rows)
    embedded = lax.dot_general(
        proj_weight, soft_rows, (((0,), (0,)), ((), ())),
        preferred_element_type=jnp.float32,
    ).astype(jnp.bfloat16)
    my_pos = seq_index * tok_rows + jnp.arange(tok_rows, dtype=jnp.int32)
    my_image = image_of(my_pos, starts)
    residual = jnp.where((my_image >= 0)[None, :], embedded, tokens.T)

    whole = exchange(residual, HEAD, head_count)
    given_residual = swapped(residual)
    along, whole, given_residual = lax.optimization_barrier((along, whole, given_residual))
    across = lax.ppermute(along, "core", [(0, 1), (1, 0)])
    half = HEAD_DIM // 2
    frequency = ROPE_BASE ** (-jnp.arange(half, dtype=jnp.float32) * 2.0 / HEAD_DIM)
    angles = my_pos.astype(jnp.float32)[:, None] * frequency[None, :]
    cosine, sine = jnp.cos(angles), jnp.sin(angles)
    gain_parts = input_gain.reshape(head_count, width, 1)
    total, row_squares = project_first(core, whole, gain_parts, along)
    queries, own = project_second(
        core,
        whole,
        gain_parts,
        across,
        total,
        row_squares,
        jnp.concatenate([cosine, cosine], axis=1),
        jnp.concatenate([-sine, sine], axis=1),
        query_gain,
        key_gain,
    )
    past_count = WINDOW // tok_rows
    near = jnp.concatenate([shifted(own, 2), shifted(own, 1)], axis=0)
    window = jnp.concatenate([shifted(near, 2), near, own, shifted(own, -1)], axis=0)
    key_pos = (seq_index - past_count) * tok_rows + jnp.arange(window.shape[0], dtype=jnp.int32)
    allowed = allowed_keys(my_pos, key_pos, starts, total_rows)
    attended = attend(
        queries.reshape(tok_rows, 1, 2, HEAD_DIM),
        window[:, :HEAD_DIM].reshape(-1, 1, HEAD_DIM),
        window[:, HEAD_DIM:].reshape(-1, 1, HEAD_DIM),
        allowed,
    )
    attended = attended.reshape(tok_rows, 2 * HEAD_DIM).T
    heads_all = exchange(attended, HEAD, head_count)
    projected, squares = project_out(core, heads_all, along, across)
    given = swapped(projected.astype(jnp.bfloat16)).astype(jnp.float32)
    all_squares = exchange(squares, ("a", "y", "core"), 16).reshape(8, 2, tok_rows)
    from_core = jnp.arange(2, dtype=jnp.int32) == lax.axis_index("a")
    squares = jnp.sum(jnp.where(from_core[None, :, None], all_squares, 0.0), axis=(0, 1))
    post = given * lax.rsqrt(squares[None, :] / D + EPSILON) * post_gain[:, None]
    return (given_residual.astype(jnp.float32) + post).astype(jnp.bfloat16).T


def solution(mesh):
    split = Mesh(mesh.devices.reshape(2, 2, Z, 4, 2), ("k", "a", "z", "y", "core"))
    seq, head = GIVEN_SEQ, GIVEN_HEAD
    return jax.shard_map(
        body,
        mesh=split,
        in_specs=(
            P(seq, head),
            P(seq, None, None),
            P(),
            P(),
            P(),
            P(None, head),
            P(),
            P(seq, head),
            P(seq, head),
            P(seq, head),
            P(),
            P(),
            P(seq, head),
            P(head),
        ),
        out_specs=P(seq, head),
        check_vma=False,
    )
```

```python
import jax
import jax.numpy as jnp
from jax import lax
from jax.experimental import pallas as pl
from jax.experimental.pallas import tpu as pltpu
from jax.sharding import Mesh
from jax.sharding import PartitionSpec as P

D = 5376
HEAD_DIM = 128
WINDOW = 1024
PATCH_SIDE = 64
POOL = 4
IMG_TOK = 256
Z = 16
ROWS_IN = 84
ROWS_OUT = 32
PAD_IN = 96
PAD_ALL = 144
WIDTH = 672

EPSILON = 1e-06
QUERY_SCALE = 168.0 ** (-0.5)
ROPE_BASE = 10000.0

GIVEN_SEQ = ("k", "a", "z")
GIVEN_HEAD = ("y", "core")
SEQ = ("k", "core", "z")
HEAD = ("y", "a")


def swapped(value):
    return lax.ppermute(value, ("a", "core"), [(0, 0), (1, 2), (2, 1), (3, 3)])


def from_half(value, flip):
    pairs = []
    for k in range(2):
        for a in range(2):
            for core in range(2):
                pairs.append(((k * 2 + a) * 2 + core, ((k ^ flip) * 2 + core) * 2 + a))
    return lax.ppermute(value, ("k", "a", "core"), pairs)


def shifted(value, steps):
    pairs = []
    for source in range(4 * Z):
        target = source + steps
        if 0 <= target < 4 * Z:
            place = [
                ((shard // (2 * Z)) * Z + shard % Z) * 2 + shard // Z % 2
                for shard in (source, target)
            ]
            pairs.append((place[0], place[1]))
    return lax.ppermute(value, ("k", "z", "core"), pairs)


def exchange(value, axes, count):
    spread = jnp.broadcast_to(value[None], (count, *value.shape))
    return lax.all_to_all(spread, axes, 0, 0, tiled=True)


def rms_scale(inputs, scale_gain):
    return (
        inputs * lax.rsqrt(jnp.mean(inputs * inputs, axis=-1, keepdims=True) + EPSILON) * scale_gain
    )


def image_of(positions, starts):
    inside = (positions[:, None] >= starts[None, :]) & (
        positions[:, None] < starts[None, :] + IMG_TOK
    )
    labels = jnp.arange(1, starts.shape[0] + 1, dtype=jnp.int32)
    return jnp.sum(jnp.where(inside, labels[None, :], 0), axis=1) - 1


def allowed_keys(query_pos, key_pos, starts, total_rows):
    query_img = image_of(query_pos, starts)
    key_img = image_of(key_pos, starts)
    inside = (key_pos >= 0) & (key_pos < total_rows)
    in_window = query_pos[:, None] - key_pos[None, :] < WINDOW
    causal = key_pos[None, :] <= query_pos[:, None]
    same_image = (query_img[:, None] == key_img[None, :]) & (query_img[:, None] >= 0)
    return inside[None, :] & in_window & (causal | same_image)


def attend(queries, key_rows, values, allowed):
    scores = jnp.einsum("qgrd,kgd->grqk", queries, key_rows, preferred_element_type=jnp.float32)
    scores = jnp.where(allowed[None, None], scores, -jnp.inf)
    row_max = jnp.max(scores, axis=-1, keepdims=True)
    weights = jnp.exp(scores - row_max)
    row_sum = jnp.sum(weights, axis=-1)
    mixed_heads = jnp.einsum(
        "grqk,kgd->qgrd", weights.astype(jnp.bfloat16), values, preferred_element_type=jnp.float32
    )
    return (mixed_heads / jnp.transpose(row_sum, (2, 0, 1))[..., None]).astype(jnp.bfloat16)


def add_part(whole_ref, gain_ref, weight_ref, block, start, squares):
    for shard in range(8):
        block[shard * ROWS_IN : (shard + 1) * ROWS_IN, :] = weight_ref[shard, 0, :ROWS_IN, :]
    part = whole_ref[0].astype(jnp.float32)
    gain = jnp.concatenate([gain_ref[0], gain_ref[0]], axis=1)
    scaled = (part * gain).astype(jnp.bfloat16)
    product = lax.dot_general(
        scaled, block[...], (((0,), (0,)), ((), ())), preferred_element_type=jnp.float32
    )
    return start + product, squares + jnp.sum(part * part, axis=0, keepdims=True)


def first_kernel(core_ref, whole_ref, gain_ref, weight_ref, total_ref, squares_ref, block):
    @pl.when(pl.program_id(0) == 0)
    def _():
        total_ref[...] = jnp.zeros_like(total_ref)
        squares_ref[...] = jnp.zeros_like(squares_ref)

    total_ref[...], squares_ref[...] = add_part(
        whole_ref, gain_ref, weight_ref, block, total_ref[...], squares_ref[...]
    )


def second_kernel(
    core_ref, whole_ref, gain_ref, weight_ref, start_ref, square_ref, cos_ref, sin_ref,
    query_gain_ref, key_gain_ref, query_ref, pair_ref, block, total, squares,
):
    step = pl.program_id(0)

    @pl.when(step == 0)
    def _():
        total[...] = start_ref[...]
        squares[...] = square_ref[...]

    total[...], squares[...] = add_part(
        whole_ref, gain_ref, weight_ref, block, total[...], squares[...]
    )

    @pl.when(step == pl.num_programs(0) - 1)
    def _():
        inverse = lax.rsqrt(squares[...] / D + EPSILON)
        inverse = jnp.transpose(jnp.broadcast_to(inverse, (HEAD_DIM, inverse.shape[1])))

        def head(index):
            return total[:, index * HEAD_DIM : (index + 1) * HEAD_DIM] * inverse

        def turned(rows, gain):
            mean_square = jnp.mean(rows * rows, axis=-1, keepdims=True)
            rows = rows * lax.rsqrt(mean_square + EPSILON) * gain
            return rows * cos_ref[...] + pltpu.roll(rows, HEAD_DIM // 2, 1) * sin_ref[...]

        for index in range(2):
            query_ref[:, index * HEAD_DIM : (index + 1) * HEAD_DIM] = (
                turned(head(index), query_gain_ref[...]) * QUERY_SCALE
            ).astype(jnp.bfloat16)
        pair_ref[:, :HEAD_DIM] = turned(head(2), key_gain_ref[...]).astype(jnp.bfloat16)
        pair_ref[:, HEAD_DIM:] = head(3).astype(jnp.bfloat16)


def own_block(step, core):
    return step // 2 * 4 + core[0] * 2 + step % 2


def other_block(step, core):
    return step // 2 * 4 + (1 - core[0]) * 2 + step % 2


def qkv_specs(block_of, width, rows):
    return [
        pl.BlockSpec((1, width, rows), lambda step, core: (block_of(step, core), 0, 0)),
        pl.BlockSpec((1, width, HEAD_DIM), lambda step, core: (block_of(step, core), 0, 0)),
        pl.BlockSpec((8, 1, PAD_IN, 512), lambda step, core: (step % 2, step // 2, 0, 0)),
    ]


def project_first(core, whole, gain, weights):
    count, width, rows = whole.shape
    fixed = lambda step, core: (0, 0)
    return pl.pallas_call(
        first_kernel,
        grid_spec=pltpu.PrefetchScalarGridSpec(
            num_scalar_prefetch=1,
            grid=(count // 2,),
            in_specs=qkv_specs(own_block, width, rows),
            out_specs=[pl.BlockSpec((rows, 512), fixed), pl.BlockSpec((1, rows), fixed)],
            scratch_shapes=[pltpu.VMEM((width, 512), jnp.bfloat16)],
        ),
        out_shape=[
            jax.ShapeDtypeStruct((rows, 512), jnp.float32),
            jax.ShapeDtypeStruct((1, rows), jnp.float32),
        ],
        compiler_params=pltpu.CompilerParams(vmem_limit_bytes=24 * 2**20),
        cost_estimate=pl.CostEstimate(
            flops=rows * 512 * D, bytes_accessed=5 * 2**20, transcendentals=0
        ),
    )(core, whole, gain, weights)


def project_second(
    core, whole, gain, weights, total, squares, cosine, sine, query_gain, key_gain
):
    count, width, rows = whole.shape
    fixed = lambda step, core: (0, 0)
    return pl.pallas_call(
        second_kernel,
        grid_spec=pltpu.PrefetchScalarGridSpec(
            num_scalar_prefetch=1,
            grid=(count // 2,),
            in_specs=qkv_specs(other_block, width, rows)
            + [
                pl.BlockSpec((rows, 512), fixed),
                pl.BlockSpec((1, rows), fixed),
                pl.BlockSpec((rows, HEAD_DIM), fixed),
                pl.BlockSpec((rows, HEAD_DIM), fixed),
                pl.BlockSpec((1, HEAD_DIM), fixed),
                pl.BlockSpec((1, HEAD_DIM), fixed),
            ],
            out_specs=[pl.BlockSpec((rows, 256), fixed), pl.BlockSpec((rows, 256), fixed)],
            scratch_shapes=[
                pltpu.VMEM((width, 512), jnp.bfloat16),
                pltpu.VMEM((rows, 512), jnp.float32),
                pltpu.VMEM((1, rows), jnp.float32),
            ],
        ),
        out_shape=[
            jax.ShapeDtypeStruct((rows, 256), jnp.bfloat16),
            jax.ShapeDtypeStruct((rows, 256), jnp.bfloat16),
        ],
        compiler_params=pltpu.CompilerParams(vmem_limit_bytes=24 * 2**20),
        cost_estimate=pl.CostEstimate(
            flops=rows * 512 * D, bytes_accessed=5 * 2**20, transcendentals=0
        ),
    )(
        core, whole, gain, weights, total, squares, cosine, sine,
        query_gain[None, :], key_gain[None, :],
    )


def out_kernel(
    core_ref, own_ref, other_ref, along_ref, across_ref, result_ref, squares_ref, total
):
    step = pl.program_id(0)

    @pl.when(step == 0)
    def _():
        total[...] = jnp.zeros_like(total)

    for heads_ref, weight_ref in ((own_ref, along_ref), (other_ref, across_ref)):
        left = weight_ref[:, 0, :ROWS_OUT, :].reshape(8 * ROWS_OUT, 512)
        right = weight_ref[:, 0, ROWS_OUT:, :]
        right = jnp.concatenate([right[:, :, :256], right[:, :, 256:]], axis=1)
        right = right.reshape(8 * ROWS_OUT, 256)
        heads = heads_ref[0]
        for first, part in ((0, left), (512, right)):
            total[first : first + part.shape[1], :] += lax.dot_general(
                part, heads, (((0,), (0,)), ((), ())), preferred_element_type=jnp.float32
            )

    @pl.when(step == pl.num_programs(0) - 1)
    def _():
        result = total[:WIDTH, :]
        result_ref[...] = result.astype(jnp.bfloat16)
        squares = jnp.sum(result * result, axis=0, keepdims=True)
        squares_ref[...] = jnp.broadcast_to(squares[None], squares_ref.shape)


def project_out(core, heads, along, across):
    count, depth, rows = heads.shape
    fixed = lambda step, core: (0, 0)
    weights = pl.BlockSpec(
        (8, 1, PAD_ALL - PAD_IN, 512), lambda step, core: (step % 2, step // 2, 2, 0)
    )
    return pl.pallas_call(
        out_kernel,
        grid_spec=pltpu.PrefetchScalarGridSpec(
            num_scalar_prefetch=1,
            grid=(count // 2,),
            in_specs=[
                pl.BlockSpec((1, depth, rows), lambda step, core: (own_block(step, core), 0, 0)),
                pl.BlockSpec((1, depth, rows), lambda step, core: (other_block(step, core), 0, 0)),
                weights,
                weights,
            ],
            out_specs=[
                pl.BlockSpec((WIDTH, rows), fixed),
                pl.BlockSpec((16, 1, rows), lambda step, core: (0, 0, 0)),
            ],
            scratch_shapes=[pltpu.VMEM((768, rows), jnp.float32)],
        ),
        out_shape=[
            jax.ShapeDtypeStruct((WIDTH, rows), jnp.bfloat16),
            jax.ShapeDtypeStruct((16, 1, rows), jnp.float32),
        ],
        compiler_params=pltpu.CompilerParams(vmem_limit_bytes=24 * 2**20),
        cost_estimate=pl.CostEstimate(
            flops=2 * rows * 768 * 2048, bytes_accessed=5 * 2**20, transcendentals=0
        ),
    )(core, heads, heads, along, across)


def body(
    tokens,
    features,
    starts,
    sources,
    soft_gain,
    proj_weight,
    input_gain,
    query_weight,
    key_weight,
    value_weight,
    query_gain,
    key_gain,
    out_weight,
    post_gain,
):
    tok_rows, width = tokens.shape
    head_count = 8
    x_count = 4
    seq_count = x_count * Z
    core_index = lax.axis_index("core")
    z_index = lax.axis_index("z")
    seq_index = lax.axis_index(SEQ)
    total_rows = seq_count * tok_rows

    out_right = jnp.pad(out_weight[:, 512:], ((0, 0), (0, 768 - width)))
    local = jnp.concatenate(
        [
            jnp.pad(
                jnp.concatenate([query_weight, key_weight, value_weight], axis=1),
                ((0, PAD_IN - ROWS_IN), (0, 0)),
            ),
            out_weight[:, :512],
            jnp.concatenate([out_right[:16], out_right[16:]], axis=1),
        ],
        axis=0,
    )
    same_half = from_half(local, 0)
    other_half = from_half(local, 1)
    k_first = lax.axis_index("k") == 0
    both = jnp.stack(
        [
            jnp.where(k_first, same_half, other_half),
            jnp.where(k_first, other_half, same_half),
        ]
    )
    core = core_index.astype(jnp.int32)[None]

    image_count = starts.shape[0]
    vis = features.shape[2]
    pooled_side = PATCH_SIDE // POOL
    pool_rows = features.shape[0] // POOL
    block_rows = pool_rows * pooled_side
    shards_each = pooled_side // pool_rows
    row = jnp.arange(block_rows, dtype=jnp.int32)
    patch = jnp.arange(features.shape[0] * PATCH_SIDE, dtype=jnp.int32)
    square = patch // (PATCH_SIDE * POOL) * pooled_side + patch % PATCH_SIDE // POOL
    ones = (row[:, None] == square[None, :]).astype(jnp.bfloat16)
    pooled = jnp.dot(
        ones, features.reshape(-1, vis), preferred_element_type=jnp.float32
    ) / (POOL * POOL)
    soft = rms_scale(pooled, soft_gain).astype(jnp.bfloat16)
    vis_part = vis // head_count
    soft_part = lax.dynamic_slice_in_dim(
        soft, lax.axis_index(GIVEN_HEAD) * vis_part, vis_part, 1
    )
    target = jnp.arange(8, dtype=jnp.int32)
    target_k, target_a, target_core = target // 4, target // 2 % 2, target % 2
    target_seq = (target_k * 2 + target_core) * Z + z_index
    frame_pos = (
        target_seq[:, None] * tok_rows + jnp.arange(tok_rows, dtype=jnp.int32)[None, :]
    ).reshape(-1)
    frame_image = image_of(frame_pos, starts)
    row_base = sources // shards_each * (block_rows * shards_each) - starts
    image_ids = jnp.arange(image_count, dtype=jnp.int32)
    frame_row = jnp.sum(
        jnp.where(frame_image[:, None] == image_ids[None, :], row_base[None, :], 0), axis=1
    )
    wanted = (frame_image >= 0) & jnp.repeat(target_a == core_index, tok_rows)
    frame_row = jnp.where(wanted, frame_row + frame_pos, -1)
    x_index = lax.axis_index(("k", "a"))
    here = x_index * (Z * block_rows) + jnp.arange(Z * block_rows, dtype=jnp.int32)
    soft_z = exchange(soft_part, "z", Z).reshape(Z * block_rows, vis_part)
    tokens = swapped(tokens)
    soft_z, both, tokens, proj_weight = lax.optimization_barrier(
        (soft_z, both, tokens, proj_weight)
    )
    along = lax.all_gather(both, "z", axis=0)
    proj_other = lax.ppermute(proj_weight, ("a", "core"), [(0, 1), (3, 2)])
    proj_weight = jnp.where(core_index == lax.axis_index("a"), proj_weight, proj_other)
    chosen = (frame_row[:, None] == here[None, :]).astype(jnp.bfloat16)
    chosen = chosen.reshape(8, tok_rows, Z * block_rows)
    frames = jnp.einsum("sk,xps->xkp", soft_z, chosen, preferred_element_type=jnp.float32)
    frames = lax.all_to_all(
        frames.astype(jnp.bfloat16), ("k", "a", "core"), 0, 0, tiled=True
    )
    mine = jnp.sum(frames.astype(jnp.float32), axis=0).astype(jnp.bfloat16)
    soft_rows = exchange(mine, HEAD, head_count).reshape(vis, tok_rows)
    gain_parts = jnp.broadcast_to(
        input_gain.reshape(head_count, width, 1), (head_count, width, HEAD_DIM)
    )
    soft_rows, gain_parts = lax.optimization_barrier((soft_rows, gain_parts))
    embedded = lax.dot_general(
        proj_weight, soft_rows, (((0,), (0,)), ((), ())),
        preferred_element_type=jnp.float32,
    ).astype(jnp.bfloat16)
    my_pos = seq_index * tok_rows + jnp.arange(tok_rows, dtype=jnp.int32)
    my_image = image_of(my_pos, starts)
    residual = jnp.where((my_image >= 0)[None, :], embedded, tokens.T)

    whole = exchange(residual, HEAD, head_count)
    along, whole = lax.optimization_barrier((along, whole))
    across = lax.ppermute(along, "core", [(0, 1), (1, 0)])
    half = HEAD_DIM // 2
    frequency = ROPE_BASE ** (-jnp.arange(half, dtype=jnp.float32) * 2.0 / HEAD_DIM)
    angles = my_pos.astype(jnp.float32)[:, None] * frequency[None, :]
    cosine, sine = jnp.cos(angles), jnp.sin(angles)
    total, row_squares = project_first(core, whole, gain_parts, along)
    queries, own = project_second(
        core,
        whole,
        gain_parts,
        across,
        total,
        row_squares,
        jnp.concatenate([cosine, cosine], axis=1),
        jnp.concatenate([-sine, sine], axis=1),
        query_gain,
        key_gain,
    )
    past_count = WINDOW // tok_rows
    near = jnp.concatenate([shifted(own, 2), shifted(own, 1)], axis=0)
    window = jnp.concatenate([shifted(near, 2), near, own, shifted(own, -1)], axis=0)
    key_pos = (seq_index - past_count) * tok_rows + jnp.arange(window.shape[0], dtype=jnp.int32)
    allowed = allowed_keys(my_pos, key_pos, starts, total_rows)
    attended = attend(
        queries.reshape(tok_rows, 1, 2, HEAD_DIM),
        window[:, :HEAD_DIM].reshape(-1, 1, HEAD_DIM),
        window[:, HEAD_DIM:].reshape(-1, 1, HEAD_DIM),
        allowed,
    )
    attended = attended.reshape(tok_rows, 2 * HEAD_DIM).T
    attended, residual = lax.optimization_barrier((attended, residual))
    given_residual = swapped(residual)
    heads_all = exchange(attended, HEAD, head_count)
    projected, squares = project_out(core, heads_all, along, across)
    given = swapped(projected).astype(jnp.float32)
    all_squares = lax.all_to_all(squares, ("a", "y", "core"), 0, 0, tiled=True)
    all_squares = all_squares.reshape(8, 2, tok_rows)
    from_core = jnp.arange(2, dtype=jnp.int32) == lax.axis_index("a")
    squares = jnp.sum(jnp.where(from_core[None, :, None], all_squares, 0.0), axis=(0, 1))
    post = given * lax.rsqrt(squares[None, :] / D + EPSILON) * post_gain[:, None]
    return (given_residual.astype(jnp.float32) + post).astype(jnp.bfloat16).T


def solution(mesh):
    split = Mesh(mesh.devices.reshape(2, 2, Z, 4, 2), ("k", "a", "z", "y", "core"))
    seq, head = GIVEN_SEQ, GIVEN_HEAD
    return jax.shard_map(
        body,
        mesh=split,
        in_specs=(
            P(seq, head),
            P(seq, None, None),
            P(),
            P(),
            P(),
            P(None, head),
            P(),
            P(seq, head),
            P(seq, head),
            P(seq, head),
            P(),
            P(),
            P(seq, head),
            P(head),
        ),
        out_specs=P(seq, head),
        check_vma=False,
    )
```

```python
import jax
import jax.numpy as jnp
from jax import lax
from jax.experimental import pallas as pl
from jax.experimental.pallas import tpu as pltpu
from jax.sharding import Mesh
from jax.sharding import PartitionSpec as P

D = 5376
HEAD_DIM = 128
WINDOW = 1024
PATCH_SIDE = 64
POOL = 4
IMG_TOK = 256
Z = 16
ROWS_IN = 84
ROWS_OUT = 32
PAD_IN = 96
PAD_ALL = 144
WIDTH = 672

EPSILON = 1e-06
QUERY_SCALE = 168.0 ** (-0.5)
ROPE_BASE = 10000.0

GIVEN_SEQ = ("k", "a", "z")
GIVEN_HEAD = ("y", "core")
SEQ = ("k", "core", "z")
HEAD = ("y", "a")


def swapped(value):
    return lax.ppermute(value, ("a", "core"), [(0, 0), (1, 2), (2, 1), (3, 3)])


def from_half(value, flip):
    pairs = []
    for k in range(2):
        for a in range(2):
            for core in range(2):
                pairs.append(((k * 2 + a) * 2 + core, ((k ^ flip) * 2 + core) * 2 + a))
    return lax.ppermute(value, ("k", "a", "core"), pairs)


def shifted(value, steps):
    pairs = []
    for source in range(4 * Z):
        target = source + steps
        if 0 <= target < 4 * Z:
            place = [
                ((shard // (2 * Z)) * Z + shard % Z) * 2 + shard // Z % 2
                for shard in (source, target)
            ]
            pairs.append((place[0], place[1]))
    return lax.ppermute(value, ("k", "z", "core"), pairs)


def exchange(value, axes, count):
    spread = jnp.broadcast_to(value[None], (count, *value.shape))
    return lax.all_to_all(spread, axes, 0, 0, tiled=True)


def rms_scale(inputs, scale_gain):
    return (
        inputs * lax.rsqrt(jnp.mean(inputs * inputs, axis=-1, keepdims=True) + EPSILON) * scale_gain
    )


def image_of(positions, starts):
    inside = (positions[:, None] >= starts[None, :]) & (
        positions[:, None] < starts[None, :] + IMG_TOK
    )
    labels = jnp.arange(1, starts.shape[0] + 1, dtype=jnp.int32)
    return jnp.sum(jnp.where(inside, labels[None, :], 0), axis=1) - 1


def allowed_keys(query_pos, key_pos, starts, total_rows):
    query_img = image_of(query_pos, starts)
    key_img = image_of(key_pos, starts)
    inside = (key_pos >= 0) & (key_pos < total_rows)
    in_window = query_pos[:, None] - key_pos[None, :] < WINDOW
    causal = key_pos[None, :] <= query_pos[:, None]
    same_image = (query_img[:, None] == key_img[None, :]) & (query_img[:, None] >= 0)
    return inside[None, :] & in_window & (causal | same_image)


def attend(queries, key_rows, values, allowed):
    scores = jnp.einsum("qgrd,kgd->grqk", queries, key_rows, preferred_element_type=jnp.float32)
    scores = jnp.where(allowed[None, None], scores, -jnp.inf)
    row_max = jnp.max(scores, axis=-1, keepdims=True)
    weights = jnp.exp(scores - row_max)
    row_sum = jnp.sum(weights, axis=-1)
    mixed_heads = jnp.einsum(
        "grqk,kgd->qgrd", weights.astype(jnp.bfloat16), values, preferred_element_type=jnp.float32
    )
    return (mixed_heads / jnp.transpose(row_sum, (2, 0, 1))[..., None]).astype(jnp.bfloat16)


def add_part(whole_ref, gain_ref, weight_ref, block, start, squares):
    for shard in range(8):
        block[shard * ROWS_IN : (shard + 1) * ROWS_IN, :] = weight_ref[shard, 0, :ROWS_IN, :]
    part = whole_ref[0].astype(jnp.float32)
    gain = jnp.transpose(gain_ref[0])[:WIDTH, :1]
    scaled = (part * gain).astype(jnp.bfloat16)
    product = lax.dot_general(
        scaled, block[...], (((0,), (0,)), ((), ())), preferred_element_type=jnp.float32
    )
    return start + product, squares + jnp.sum(part * part, axis=0, keepdims=True)


def first_kernel(core_ref, whole_ref, gain_ref, weight_ref, total_ref, squares_ref, block):
    @pl.when(pl.program_id(0) == 0)
    def _():
        total_ref[...] = jnp.zeros_like(total_ref)
        squares_ref[...] = jnp.zeros_like(squares_ref)

    total_ref[...], squares_ref[...] = add_part(
        whole_ref, gain_ref, weight_ref, block, total_ref[...], squares_ref[...]
    )


def second_kernel(
    core_ref, whole_ref, gain_ref, weight_ref, start_ref, square_ref, cos_ref, sin_ref,
    query_gain_ref, key_gain_ref, query_ref, pair_ref, block, total, squares,
):
    step = pl.program_id(0)

    @pl.when(step == 0)
    def _():
        total[...] = start_ref[...]
        squares[...] = square_ref[...]

    total[...], squares[...] = add_part(
        whole_ref, gain_ref, weight_ref, block, total[...], squares[...]
    )

    @pl.when(step == pl.num_programs(0) - 1)
    def _():
        inverse = lax.rsqrt(squares[...] / D + EPSILON)
        inverse = jnp.transpose(jnp.broadcast_to(inverse, (HEAD_DIM, inverse.shape[1])))

        def head(index):
            return total[:, index * HEAD_DIM : (index + 1) * HEAD_DIM] * inverse

        def turned(rows, gain):
            mean_square = jnp.mean(rows * rows, axis=-1, keepdims=True)
            rows = rows * lax.rsqrt(mean_square + EPSILON) * gain
            return rows * cos_ref[...] + pltpu.roll(rows, HEAD_DIM // 2, 1) * sin_ref[...]

        for index in range(2):
            query_ref[:, index * HEAD_DIM : (index + 1) * HEAD_DIM] = (
                turned(head(index), query_gain_ref[...]) * QUERY_SCALE
            ).astype(jnp.bfloat16)
        pair_ref[:, :HEAD_DIM] = turned(head(2), key_gain_ref[...]).astype(jnp.bfloat16)
        pair_ref[:, HEAD_DIM:] = head(3).astype(jnp.bfloat16)


def own_block(step, core):
    return step // 2 * 4 + core[0] * 2 + step % 2


def other_block(step, core):
    return step // 2 * 4 + (1 - core[0]) * 2 + step % 2


def qkv_specs(block_of, width, rows):
    return [
        pl.BlockSpec((1, width, rows), lambda step, core: (block_of(step, core), 0, 0)),
        pl.BlockSpec((1, 8, 768), lambda step, core: (block_of(step, core), 0, 0)),
        pl.BlockSpec((8, 1, PAD_IN, 512), lambda step, core: (step % 2, step // 2, 0, 0)),
    ]


def project_first(core, whole, gain, weights):
    count, width, rows = whole.shape
    fixed = lambda step, core: (0, 0)
    return pl.pallas_call(
        first_kernel,
        grid_spec=pltpu.PrefetchScalarGridSpec(
            num_scalar_prefetch=1,
            grid=(count // 2,),
            in_specs=qkv_specs(own_block, width, rows),
            out_specs=[pl.BlockSpec((rows, 512), fixed), pl.BlockSpec((1, rows), fixed)],
            scratch_shapes=[pltpu.VMEM((width, 512), jnp.bfloat16)],
        ),
        out_shape=[
            jax.ShapeDtypeStruct((rows, 512), jnp.float32),
            jax.ShapeDtypeStruct((1, rows), jnp.float32),
        ],
        compiler_params=pltpu.CompilerParams(vmem_limit_bytes=24 * 2**20),
        cost_estimate=pl.CostEstimate(
            flops=rows * 512 * D, bytes_accessed=5 * 2**20, transcendentals=0
        ),
    )(core, whole, gain, weights)


def project_second(
    core, whole, gain, weights, total, squares, cosine, sine, query_gain, key_gain
):
    count, width, rows = whole.shape
    fixed = lambda step, core: (0, 0)
    return pl.pallas_call(
        second_kernel,
        grid_spec=pltpu.PrefetchScalarGridSpec(
            num_scalar_prefetch=1,
            grid=(count // 2,),
            in_specs=qkv_specs(other_block, width, rows)
            + [
                pl.BlockSpec((rows, 512), fixed),
                pl.BlockSpec((1, rows), fixed),
                pl.BlockSpec((rows, HEAD_DIM), fixed),
                pl.BlockSpec((rows, HEAD_DIM), fixed),
                pl.BlockSpec((1, HEAD_DIM), fixed),
                pl.BlockSpec((1, HEAD_DIM), fixed),
            ],
            out_specs=[pl.BlockSpec((rows, 256), fixed), pl.BlockSpec((rows, 256), fixed)],
            scratch_shapes=[
                pltpu.VMEM((width, 512), jnp.bfloat16),
                pltpu.VMEM((rows, 512), jnp.float32),
                pltpu.VMEM((1, rows), jnp.float32),
            ],
        ),
        out_shape=[
            jax.ShapeDtypeStruct((rows, 256), jnp.bfloat16),
            jax.ShapeDtypeStruct((rows, 256), jnp.bfloat16),
        ],
        compiler_params=pltpu.CompilerParams(vmem_limit_bytes=24 * 2**20),
        cost_estimate=pl.CostEstimate(
            flops=rows * 512 * D, bytes_accessed=5 * 2**20, transcendentals=0
        ),
    )(
        core, whole, gain, weights, total, squares, cosine, sine,
        query_gain[None, :], key_gain[None, :],
    )


def out_kernel(
    core_ref, own_ref, other_ref, along_ref, across_ref, result_ref, squares_ref, total
):
    step = pl.program_id(0)

    @pl.when(step == 0)
    def _():
        total[...] = jnp.zeros_like(total)

    for heads_ref, weight_ref in ((own_ref, along_ref), (other_ref, across_ref)):
        left = weight_ref[:, 0, :ROWS_OUT, :].reshape(8 * ROWS_OUT, 512)
        right = weight_ref[:, 0, ROWS_OUT:, :]
        right = jnp.concatenate([right[:, :, :256], right[:, :, 256:]], axis=1)
        right = right.reshape(8 * ROWS_OUT, 256)
        heads = heads_ref[0]
        for first, part in ((0, left), (512, right)):
            total[first : first + part.shape[1], :] += lax.dot_general(
                part, heads, (((0,), (0,)), ((), ())), preferred_element_type=jnp.float32
            )

    @pl.when(step == pl.num_programs(0) - 1)
    def _():
        result = total[:WIDTH, :]
        result_ref[...] = result.astype(jnp.bfloat16)
        squares = jnp.sum(result * result, axis=0, keepdims=True)
        squares_ref[...] = jnp.broadcast_to(squares[None], squares_ref.shape)


def project_out(core, heads, along, across):
    count, depth, rows = heads.shape
    fixed = lambda step, core: (0, 0)
    weights = pl.BlockSpec(
        (8, 1, PAD_ALL - PAD_IN, 512), lambda step, core: (step % 2, step // 2, 2, 0)
    )
    return pl.pallas_call(
        out_kernel,
        grid_spec=pltpu.PrefetchScalarGridSpec(
            num_scalar_prefetch=1,
            grid=(count // 2,),
            in_specs=[
                pl.BlockSpec((1, depth, rows), lambda step, core: (own_block(step, core), 0, 0)),
                pl.BlockSpec((1, depth, rows), lambda step, core: (other_block(step, core), 0, 0)),
                weights,
                weights,
            ],
            out_specs=[
                pl.BlockSpec((WIDTH, rows), fixed),
                pl.BlockSpec((16, 1, rows), lambda step, core: (0, 0, 0)),
            ],
            scratch_shapes=[pltpu.VMEM((768, rows), jnp.float32)],
        ),
        out_shape=[
            jax.ShapeDtypeStruct((WIDTH, rows), jnp.bfloat16),
            jax.ShapeDtypeStruct((16, 1, rows), jnp.float32),
        ],
        compiler_params=pltpu.CompilerParams(vmem_limit_bytes=24 * 2**20),
        cost_estimate=pl.CostEstimate(
            flops=2 * rows * 768 * 2048, bytes_accessed=5 * 2**20, transcendentals=0
        ),
    )(core, heads, heads, along, across)


def body(
    tokens,
    features,
    starts,
    sources,
    soft_gain,
    proj_weight,
    input_gain,
    query_weight,
    key_weight,
    value_weight,
    query_gain,
    key_gain,
    out_weight,
    post_gain,
):
    tok_rows, width = tokens.shape
    head_count = 8
    x_count = 4
    seq_count = x_count * Z
    core_index = lax.axis_index("core")
    z_index = lax.axis_index("z")
    seq_index = lax.axis_index(SEQ)
    total_rows = seq_count * tok_rows

    out_right = jnp.pad(out_weight[:, 512:], ((0, 0), (0, 768 - width)))
    local = jnp.concatenate(
        [
            jnp.pad(
                jnp.concatenate([query_weight, key_weight, value_weight], axis=1),
                ((0, PAD_IN - ROWS_IN), (0, 0)),
            ),
            out_weight[:, :512],
            jnp.concatenate([out_right[:16], out_right[16:]], axis=1),
        ],
        axis=0,
    )
    same_half = from_half(local, 0)
    other_half = from_half(local, 1)
    k_first = lax.axis_index("k") == 0
    both = jnp.stack(
        [
            jnp.where(k_first, same_half, other_half),
            jnp.where(k_first, other_half, same_half),
        ]
    )
    core = core_index.astype(jnp.int32)[None]

    image_count = starts.shape[0]
    vis = features.shape[2]
    pooled_side = PATCH_SIDE // POOL
    pool_rows = features.shape[0] // POOL
    block_rows = pool_rows * pooled_side
    shards_each = pooled_side // pool_rows
    row = jnp.arange(block_rows, dtype=jnp.int32)
    patch = jnp.arange(features.shape[0] * PATCH_SIDE, dtype=jnp.int32)
    square = patch // (PATCH_SIDE * POOL) * pooled_side + patch % PATCH_SIDE // POOL
    ones = (row[:, None] == square[None, :]).astype(jnp.bfloat16)
    pooled = jnp.dot(
        ones, features.reshape(-1, vis), preferred_element_type=jnp.float32
    ) / (POOL * POOL)
    soft = rms_scale(pooled, soft_gain).astype(jnp.bfloat16)
    vis_part = vis // head_count
    soft_part = lax.dynamic_slice_in_dim(
        soft, lax.axis_index(GIVEN_HEAD) * vis_part, vis_part, 1
    )
    target = jnp.arange(8, dtype=jnp.int32)
    target_k, target_a, target_core = target // 4, target // 2 % 2, target % 2
    target_seq = (target_k * 2 + target_core) * Z + z_index
    frame_pos = (
        target_seq[:, None] * tok_rows + jnp.arange(tok_rows, dtype=jnp.int32)[None, :]
    ).reshape(-1)
    frame_image = image_of(frame_pos, starts)
    row_base = sources // shards_each * (block_rows * shards_each) - starts
    image_ids = jnp.arange(image_count, dtype=jnp.int32)
    frame_row = jnp.sum(
        jnp.where(frame_image[:, None] == image_ids[None, :], row_base[None, :], 0), axis=1
    )
    wanted = (frame_image >= 0) & jnp.repeat(target_a == core_index, tok_rows)
    frame_row = jnp.where(wanted, frame_row + frame_pos, -1)
    x_index = lax.axis_index(("k", "a"))
    here = x_index * (Z * block_rows) + jnp.arange(Z * block_rows, dtype=jnp.int32)
    soft_z = exchange(soft_part, "z", Z).reshape(Z * block_rows, vis_part)
    tokens = swapped(tokens)
    soft_z, both, tokens, proj_weight = lax.optimization_barrier(
        (soft_z, both, tokens, proj_weight)
    )
    along = lax.all_gather(both, "z", axis=0)
    proj_other = lax.ppermute(proj_weight, ("a", "core"), [(0, 1), (3, 2)])
    proj_weight = jnp.where(core_index == lax.axis_index("a"), proj_weight, proj_other)
    chosen = (frame_row[:, None] == here[None, :]).astype(jnp.bfloat16)
    chosen = chosen.reshape(8, tok_rows, Z * block_rows)
    frames = jnp.einsum("sk,xps->xkp", soft_z, chosen, preferred_element_type=jnp.float32)
    frames = lax.all_to_all(
        frames.astype(jnp.bfloat16), ("k", "a", "core"), 0, 0, tiled=True
    )
    mine = jnp.sum(frames.astype(jnp.float32), axis=0).astype(jnp.bfloat16)
    soft_rows = exchange(mine, HEAD, head_count).reshape(vis, tok_rows)
    gain_parts = jnp.broadcast_to(
        jnp.pad(input_gain.reshape(head_count, 1, width), ((0, 0), (0, 0), (0, 768 - width))),
        (head_count, 8, 768),
    )
    embedded = lax.dot_general(
        proj_weight, soft_rows, (((0,), (0,)), ((), ())),
        preferred_element_type=jnp.float32,
    ).astype(jnp.bfloat16)
    my_pos = seq_index * tok_rows + jnp.arange(tok_rows, dtype=jnp.int32)
    my_image = image_of(my_pos, starts)
    residual = jnp.where((my_image >= 0)[None, :], embedded, tokens.T)

    whole = exchange(residual, HEAD, head_count)
    given_residual = swapped(residual)
    along, whole, given_residual = lax.optimization_barrier((along, whole, given_residual))
    across = lax.ppermute(along, "core", [(0, 1), (1, 0)])
    half = HEAD_DIM // 2
    frequency = ROPE_BASE ** (-jnp.arange(half, dtype=jnp.float32) * 2.0 / HEAD_DIM)
    angles = my_pos.astype(jnp.float32)[:, None] * frequency[None, :]
    cosine, sine = jnp.cos(angles), jnp.sin(angles)
    total, row_squares = project_first(core, whole, gain_parts, along)
    queries, own = project_second(
        core,
        whole,
        gain_parts,
        across,
        total,
        row_squares,
        jnp.concatenate([cosine, cosine], axis=1),
        jnp.concatenate([-sine, sine], axis=1),
        query_gain,
        key_gain,
    )
    past_count = WINDOW // tok_rows
    near = jnp.concatenate([shifted(own, 2), shifted(own, 1)], axis=0)
    window = jnp.concatenate([shifted(near, 2), near, own, shifted(own, -1)], axis=0)
    key_pos = (seq_index - past_count) * tok_rows + jnp.arange(window.shape[0], dtype=jnp.int32)
    allowed = allowed_keys(my_pos, key_pos, starts, total_rows)
    attended = attend(
        queries.reshape(tok_rows, 1, 2, HEAD_DIM),
        window[:, :HEAD_DIM].reshape(-1, 1, HEAD_DIM),
        window[:, HEAD_DIM:].reshape(-1, 1, HEAD_DIM),
        allowed,
    )
    attended = attended.reshape(tok_rows, 2 * HEAD_DIM).T
    heads_all = exchange(attended, HEAD, head_count)
    projected, squares = project_out(core, heads_all, along, across)
    given = swapped(projected).astype(jnp.float32)
    all_squares = lax.all_to_all(squares, ("a", "y", "core"), 0, 0, tiled=True)
    all_squares = all_squares.reshape(8, 2, tok_rows)
    from_core = jnp.arange(2, dtype=jnp.int32) == lax.axis_index("a")
    squares = jnp.sum(jnp.where(from_core[None, :, None], all_squares, 0.0), axis=(0, 1))
    post = given * lax.rsqrt(squares[None, :] / D + EPSILON) * post_gain[:, None]
    return (given_residual.astype(jnp.float32) + post).astype(jnp.bfloat16).T


def solution(mesh):
    split = Mesh(mesh.devices.reshape(2, 2, Z, 4, 2), ("k", "a", "z", "y", "core"))
    seq, head = GIVEN_SEQ, GIVEN_HEAD
    return jax.shard_map(
        body,
        mesh=split,
        in_specs=(
            P(seq, head),
            P(seq, None, None),
            P(),
            P(),
            P(),
            P(None, head),
            P(),
            P(seq, head),
            P(seq, head),
            P(seq, head),
            P(),
            P(),
            P(seq, head),
            P(head),
        ),
        out_specs=P(seq, head),
        check_vma=False,
    )
```

```python
import jax
import jax.numpy as jnp
from jax import lax
from jax.experimental import pallas as pl
from jax.experimental.pallas import tpu as pltpu
from jax.sharding import Mesh
from jax.sharding import PartitionSpec as P

D = 5376
HEAD_DIM = 128
WINDOW = 1024
PATCH_SIDE = 64
POOL = 4
IMG_TOK = 256
Z = 16
ROWS_IN = 84
ROWS_OUT = 32
PAD_IN = 96
PAD_ALL = 144
WIDTH = 672

EPSILON = 1e-06
QUERY_SCALE = 168.0 ** (-0.5)
ROPE_BASE = 10000.0

GIVEN_SEQ = ("k", "a", "z")
GIVEN_HEAD = ("y", "core")
SEQ = ("k", "core", "z")
HEAD = ("y", "a")


def swapped(value):
    return lax.ppermute(value, ("a", "core"), [(0, 0), (1, 2), (2, 1), (3, 3)])


def from_half(value, flip):
    pairs = []
    for k in range(2):
        for a in range(2):
            for core in range(2):
                pairs.append(((k * 2 + a) * 2 + core, ((k ^ flip) * 2 + core) * 2 + a))
    return lax.ppermute(value, ("k", "a", "core"), pairs)


def shifted(value, steps):
    pairs = []
    for source in range(4 * Z):
        target = source + steps
        if 0 <= target < 4 * Z:
            place = [
                ((shard // (2 * Z)) * Z + shard % Z) * 2 + shard // Z % 2
                for shard in (source, target)
            ]
            pairs.append((place[0], place[1]))
    return lax.ppermute(value, ("k", "z", "core"), pairs)


def exchange(value, axes, count):
    spread = jnp.broadcast_to(value[None], (count, *value.shape))
    return lax.all_to_all(spread, axes, 0, 0, tiled=True)


def rms_scale(inputs, scale_gain):
    return (
        inputs * lax.rsqrt(jnp.mean(inputs * inputs, axis=-1, keepdims=True) + EPSILON) * scale_gain
    )


def image_of(positions, starts):
    inside = (positions[:, None] >= starts[None, :]) & (
        positions[:, None] < starts[None, :] + IMG_TOK
    )
    labels = jnp.arange(1, starts.shape[0] + 1, dtype=jnp.int32)
    return jnp.sum(jnp.where(inside, labels[None, :], 0), axis=1) - 1


def allowed_keys(query_pos, key_pos, starts, total_rows):
    query_img = image_of(query_pos, starts)
    key_img = image_of(key_pos, starts)
    inside = (key_pos >= 0) & (key_pos < total_rows)
    in_window = query_pos[:, None] - key_pos[None, :] < WINDOW
    causal = key_pos[None, :] <= query_pos[:, None]
    same_image = (query_img[:, None] == key_img[None, :]) & (query_img[:, None] >= 0)
    return inside[None, :] & in_window & (causal | same_image)


def attend(queries, key_rows, values, allowed):
    scores = jnp.einsum("qgrd,kgd->grqk", queries, key_rows, preferred_element_type=jnp.float32)
    scores = jnp.where(allowed[None, None], scores, -jnp.inf)
    row_max = jnp.max(scores, axis=-1, keepdims=True)
    weights = jnp.exp(scores - row_max)
    row_sum = jnp.sum(weights, axis=-1)
    mixed_heads = jnp.einsum(
        "grqk,kgd->qgrd", weights.astype(jnp.bfloat16), values, preferred_element_type=jnp.float32
    )
    return (mixed_heads / jnp.transpose(row_sum, (2, 0, 1))[..., None]).astype(jnp.bfloat16)


def add_part(whole_ref, gain_ref, weight_ref, block, start, squares):
    for shard in range(8):
        block[shard * ROWS_IN : (shard + 1) * ROWS_IN, :] = weight_ref[shard, 0, :ROWS_IN, :]
    part = whole_ref[0].astype(jnp.float32)
    gain = jnp.concatenate([gain_ref[0], gain_ref[0]], axis=1)
    scaled = (part * gain).astype(jnp.bfloat16)
    product = lax.dot_general(
        scaled, block[...], (((0,), (0,)), ((), ())), preferred_element_type=jnp.float32
    )
    return start + product, squares + jnp.sum(part * part, axis=0, keepdims=True)


def first_kernel(core_ref, whole_ref, gain_ref, weight_ref, total_ref, squares_ref, block):
    @pl.when(pl.program_id(0) == 0)
    def _():
        total_ref[...] = jnp.zeros_like(total_ref)
        squares_ref[...] = jnp.zeros_like(squares_ref)

    total_ref[...], squares_ref[...] = add_part(
        whole_ref, gain_ref, weight_ref, block, total_ref[...], squares_ref[...]
    )


def second_kernel(
    core_ref, whole_ref, gain_ref, weight_ref, start_ref, square_ref, cos_ref, sin_ref,
    query_gain_ref, key_gain_ref, query_ref, pair_ref, block, total, squares,
):
    step = pl.program_id(0)

    @pl.when(step == 0)
    def _():
        total[...] = start_ref[...]
        squares[...] = square_ref[...]

    total[...], squares[...] = add_part(
        whole_ref, gain_ref, weight_ref, block, total[...], squares[...]
    )

    @pl.when(step == pl.num_programs(0) - 1)
    def _():
        inverse = lax.rsqrt(squares[...] / D + EPSILON)
        inverse = jnp.transpose(jnp.broadcast_to(inverse, (HEAD_DIM, inverse.shape[1])))

        def head(index):
            return total[:, index * HEAD_DIM : (index + 1) * HEAD_DIM] * inverse

        def turned(rows, gain):
            mean_square = jnp.mean(rows * rows, axis=-1, keepdims=True)
            rows = rows * lax.rsqrt(mean_square + EPSILON) * gain
            return rows * cos_ref[...] + pltpu.roll(rows, HEAD_DIM // 2, 1) * sin_ref[...]

        for index in range(2):
            query_ref[:, index * HEAD_DIM : (index + 1) * HEAD_DIM] = (
                turned(head(index), query_gain_ref[...]) * QUERY_SCALE
            ).astype(jnp.bfloat16)
        pair_ref[:, :HEAD_DIM] = turned(head(2), key_gain_ref[...]).astype(jnp.bfloat16)
        pair_ref[:, HEAD_DIM:] = head(3).astype(jnp.bfloat16)


def own_block(step, core):
    return step // 2 * 4 + core[0] * 2 + step % 2


def other_block(step, core):
    return step // 2 * 4 + (1 - core[0]) * 2 + step % 2


def qkv_specs(block_of, width, rows):
    return [
        pl.BlockSpec((1, width, rows), lambda step, core: (block_of(step, core), 0, 0)),
        pl.BlockSpec((1, width, HEAD_DIM), lambda step, core: (block_of(step, core), 0, 0)),
        pl.BlockSpec((8, 1, PAD_IN, 512), lambda step, core: (step % 2, step // 2, 0, 0)),
    ]


def project_first(core, whole, gain, weights):
    count, width, rows = whole.shape
    fixed = lambda step, core: (0, 0)
    return pl.pallas_call(
        first_kernel,
        grid_spec=pltpu.PrefetchScalarGridSpec(
            num_scalar_prefetch=1,
            grid=(count // 2,),
            in_specs=qkv_specs(own_block, width, rows),
            out_specs=[pl.BlockSpec((rows, 512), fixed), pl.BlockSpec((1, rows), fixed)],
            scratch_shapes=[pltpu.VMEM((width, 512), jnp.bfloat16)],
        ),
        out_shape=[
            jax.ShapeDtypeStruct((rows, 512), jnp.float32),
            jax.ShapeDtypeStruct((1, rows), jnp.float32),
        ],
        compiler_params=pltpu.CompilerParams(vmem_limit_bytes=24 * 2**20),
        cost_estimate=pl.CostEstimate(
            flops=rows * 512 * D, bytes_accessed=5 * 2**20, transcendentals=0
        ),
    )(core, whole, gain, weights)


def project_second(
    core, whole, gain, weights, total, squares, cosine, sine, query_gain, key_gain
):
    count, width, rows = whole.shape
    fixed = lambda step, core: (0, 0)
    return pl.pallas_call(
        second_kernel,
        grid_spec=pltpu.PrefetchScalarGridSpec(
            num_scalar_prefetch=1,
            grid=(count // 2,),
            in_specs=qkv_specs(other_block, width, rows)
            + [
                pl.BlockSpec((rows, 512), fixed),
                pl.BlockSpec((1, rows), fixed),
                pl.BlockSpec((rows, HEAD_DIM), fixed),
                pl.BlockSpec((rows, HEAD_DIM), fixed),
                pl.BlockSpec((1, HEAD_DIM), fixed),
                pl.BlockSpec((1, HEAD_DIM), fixed),
            ],
            out_specs=[pl.BlockSpec((rows, 256), fixed), pl.BlockSpec((rows, 256), fixed)],
            scratch_shapes=[
                pltpu.VMEM((width, 512), jnp.bfloat16),
                pltpu.VMEM((rows, 512), jnp.float32),
                pltpu.VMEM((1, rows), jnp.float32),
            ],
        ),
        out_shape=[
            jax.ShapeDtypeStruct((rows, 256), jnp.bfloat16),
            jax.ShapeDtypeStruct((rows, 256), jnp.bfloat16),
        ],
        compiler_params=pltpu.CompilerParams(vmem_limit_bytes=24 * 2**20),
        cost_estimate=pl.CostEstimate(
            flops=rows * 512 * D, bytes_accessed=5 * 2**20, transcendentals=0
        ),
    )(
        core, whole, gain, weights, total, squares, cosine, sine,
        query_gain[None, :], key_gain[None, :],
    )


def out_kernel(
    core_ref, own_ref, other_ref, along_ref, across_ref, result_ref, squares_ref, total
):
    step = pl.program_id(0)

    @pl.when(step == 0)
    def _():
        total[...] = jnp.zeros_like(total)

    for heads_ref, weight_ref in ((own_ref, along_ref), (other_ref, across_ref)):
        left = weight_ref[:, 0, :ROWS_OUT, :].reshape(8 * ROWS_OUT, 512)
        right = weight_ref[:, 0, ROWS_OUT:, :]
        right = jnp.concatenate([right[:, :, :256], right[:, :, 256:]], axis=1)
        right = right.reshape(8 * ROWS_OUT, 256)
        heads = heads_ref[0]
        for first, part in ((0, left), (512, right)):
            total[first : first + part.shape[1], :] += lax.dot_general(
                part, heads, (((0,), (0,)), ((), ())), preferred_element_type=jnp.float32
            )

    @pl.when(step == pl.num_programs(0) - 1)
    def _():
        result = total[:WIDTH, :]
        result_ref[...] = result.astype(jnp.bfloat16)
        squares = jnp.sum(result * result, axis=0, keepdims=True)
        squares_ref[...] = jnp.broadcast_to(squares[None], squares_ref.shape)


def project_out(core, heads, along, across):
    count, depth, rows = heads.shape
    fixed = lambda step, core: (0, 0)
    weights = pl.BlockSpec(
        (8, 1, PAD_ALL - PAD_IN, 512), lambda step, core: (step % 2, step // 2, 2, 0)
    )
    return pl.pallas_call(
        out_kernel,
        grid_spec=pltpu.PrefetchScalarGridSpec(
            num_scalar_prefetch=1,
            grid=(count // 2,),
            in_specs=[
                pl.BlockSpec((1, depth, rows), lambda step, core: (own_block(step, core), 0, 0)),
                pl.BlockSpec((1, depth, rows), lambda step, core: (other_block(step, core), 0, 0)),
                weights,
                weights,
            ],
            out_specs=[
                pl.BlockSpec((WIDTH, rows), fixed),
                pl.BlockSpec((16, 1, rows), lambda step, core: (0, 0, 0)),
            ],
            scratch_shapes=[pltpu.VMEM((768, rows), jnp.float32)],
        ),
        out_shape=[
            jax.ShapeDtypeStruct((WIDTH, rows), jnp.bfloat16),
            jax.ShapeDtypeStruct((16, 1, rows), jnp.float32),
        ],
        compiler_params=pltpu.CompilerParams(vmem_limit_bytes=24 * 2**20),
        cost_estimate=pl.CostEstimate(
            flops=2 * rows * 768 * 2048, bytes_accessed=5 * 2**20, transcendentals=0
        ),
    )(core, heads, heads, along, across)


def body(
    tokens,
    features,
    starts,
    sources,
    soft_gain,
    proj_weight,
    input_gain,
    query_weight,
    key_weight,
    value_weight,
    query_gain,
    key_gain,
    out_weight,
    post_gain,
):
    tok_rows, width = tokens.shape
    head_count = 8
    x_count = 4
    seq_count = x_count * Z
    core_index = lax.axis_index("core")
    z_index = lax.axis_index("z")
    seq_index = lax.axis_index(SEQ)
    total_rows = seq_count * tok_rows

    out_right = jnp.pad(out_weight[:, 512:], ((0, 0), (0, 768 - width)))
    local = jnp.concatenate(
        [
            jnp.pad(
                jnp.concatenate([query_weight, key_weight, value_weight], axis=1),
                ((0, PAD_IN - ROWS_IN), (0, 0)),
            ),
            out_weight[:, :512],
            jnp.concatenate([out_right[:16], out_right[16:]], axis=1),
        ],
        axis=0,
    )
    same_half = from_half(local, 0)
    other_half = from_half(local, 1)
    k_first = lax.axis_index("k") == 0
    both = jnp.stack(
        [
            jnp.where(k_first, same_half, other_half),
            jnp.where(k_first, other_half, same_half),
        ]
    )
    core = core_index.astype(jnp.int32)[None]

    image_count = starts.shape[0]
    vis = features.shape[2]
    pooled_side = PATCH_SIDE // POOL
    pool_rows = features.shape[0] // POOL
    block_rows = pool_rows * pooled_side
    shards_each = pooled_side // pool_rows
    row = jnp.arange(block_rows, dtype=jnp.int32)
    patch = jnp.arange(features.shape[0] * PATCH_SIDE, dtype=jnp.int32)
    square = patch // (PATCH_SIDE * POOL) * pooled_side + patch % PATCH_SIDE // POOL
    ones = (row[:, None] == square[None, :]).astype(jnp.bfloat16)
    pooled = jnp.dot(
        ones, features.reshape(-1, vis), preferred_element_type=jnp.float32
    ) / (POOL * POOL)
    soft = rms_scale(pooled, soft_gain).astype(jnp.bfloat16)
    vis_part = vis // head_count
    soft_part = lax.dynamic_slice_in_dim(
        soft, lax.axis_index(GIVEN_HEAD) * vis_part, vis_part, 1
    )
    target = jnp.arange(8, dtype=jnp.int32)
    target_k, target_a, target_core = target // 4, target // 2 % 2, target % 2
    target_seq = (target_k * 2 + target_core) * Z + z_index
    frame_pos = (
        target_seq[:, None] * tok_rows + jnp.arange(tok_rows, dtype=jnp.int32)[None, :]
    ).reshape(-1)
    frame_image = image_of(frame_pos, starts)
    row_base = sources // shards_each * (block_rows * shards_each) - starts
    image_ids = jnp.arange(image_count, dtype=jnp.int32)
    frame_row = jnp.sum(
        jnp.where(frame_image[:, None] == image_ids[None, :], row_base[None, :], 0), axis=1
    )
    wanted = (frame_image >= 0) & jnp.repeat(target_a == core_index, tok_rows)
    frame_row = jnp.where(wanted, frame_row + frame_pos, -1)
    x_index = lax.axis_index(("k", "a"))
    here = x_index * (Z * block_rows) + jnp.arange(Z * block_rows, dtype=jnp.int32)
    soft_z = exchange(soft_part, "z", Z).reshape(Z * block_rows, vis_part)
    tokens = swapped(tokens)
    soft_z, both, tokens, proj_weight = lax.optimization_barrier(
        (soft_z, both, tokens, proj_weight)
    )
    along = lax.all_gather(both, "z", axis=0)
    proj_other = lax.ppermute(proj_weight, ("a", "core"), [(0, 1), (3, 2)])
    proj_weight = jnp.where(core_index == lax.axis_index("a"), proj_weight, proj_other)
    chosen = (frame_row[:, None] == here[None, :]).astype(jnp.bfloat16)
    chosen = chosen.reshape(8, tok_rows, Z * block_rows)
    frames = jnp.einsum("sk,xps->xkp", soft_z, chosen, preferred_element_type=jnp.float32)
    frames = lax.all_to_all(
        frames.astype(jnp.bfloat16), ("k", "a", "core"), 0, 0, tiled=True
    )
    mine = jnp.sum(frames.astype(jnp.float32), axis=0).astype(jnp.bfloat16)
    soft_rows = exchange(mine, HEAD, head_count).reshape(vis, tok_rows)
    gain_parts = jnp.broadcast_to(
        input_gain.reshape(head_count, width, 1), (head_count, width, HEAD_DIM)
    )
    embedded = lax.dot_general(
        proj_weight, soft_rows, (((0,), (0,)), ((), ())),
        preferred_element_type=jnp.float32,
    ).astype(jnp.bfloat16)
    my_pos = seq_index * tok_rows + jnp.arange(tok_rows, dtype=jnp.int32)
    my_image = image_of(my_pos, starts)
    residual = jnp.where((my_image >= 0)[None, :], embedded, tokens.T)

    whole = exchange(residual, HEAD, head_count)
    given_residual = swapped(residual)
    along, whole, given_residual = lax.optimization_barrier((along, whole, given_residual))
    across = lax.ppermute(along, "core", [(0, 1), (1, 0)])
    half = HEAD_DIM // 2
    frequency = ROPE_BASE ** (-jnp.arange(half, dtype=jnp.float32) * 2.0 / HEAD_DIM)
    angles = my_pos.astype(jnp.float32)[:, None] * frequency[None, :]
    cosine, sine = jnp.cos(angles), jnp.sin(angles)
    total, row_squares = project_first(core, whole, gain_parts, along)
    queries, own = project_second(
        core,
        whole,
        gain_parts,
        across,
        total,
        row_squares,
        jnp.concatenate([cosine, cosine], axis=1),
        jnp.concatenate([-sine, sine], axis=1),
        query_gain,
        key_gain,
    )
    past_count = WINDOW // tok_rows
    near = jnp.concatenate([shifted(own, 2), shifted(own, 1)], axis=0)
    window = jnp.concatenate([shifted(near, 2), near, own, shifted(own, -1)], axis=0)
    key_pos = (seq_index - past_count) * tok_rows + jnp.arange(window.shape[0], dtype=jnp.int32)
    allowed = allowed_keys(my_pos, key_pos, starts, total_rows)
    attended = attend(
        queries.reshape(tok_rows, 1, 2, HEAD_DIM),
        window[:, :HEAD_DIM].reshape(-1, 1, HEAD_DIM),
        window[:, HEAD_DIM:].reshape(-1, 1, HEAD_DIM),
        allowed,
    )
    attended = attended.reshape(tok_rows, 2 * HEAD_DIM).T
    heads_all = exchange(attended, HEAD, head_count)
    projected, squares = project_out(core, heads_all, along, across)
    given = swapped(projected).astype(jnp.float32)
    all_squares = lax.all_to_all(squares, ("a", "y", "core"), 0, 0, tiled=True)
    all_squares = all_squares.reshape(8, 2, tok_rows)
    from_core = jnp.arange(2, dtype=jnp.int32) == lax.axis_index("a")
    squares = jnp.sum(jnp.where(from_core[None, :, None], all_squares, 0.0), axis=(0, 1))
    post = given * lax.rsqrt(squares[None, :] / D + EPSILON) * post_gain[:, None]
    return (given_residual.astype(jnp.float32) + post).astype(jnp.bfloat16).T


def solution(mesh):
    split = Mesh(mesh.devices.reshape(2, 2, Z, 4, 2), ("k", "a", "z", "y", "core"))
    seq, head = GIVEN_SEQ, GIVEN_HEAD
    return jax.shard_map(
        body,
        mesh=split,
        in_specs=(
            P(seq, head),
            P(seq, None, None),
            P(),
            P(),
            P(),
            P(None, head),
            P(),
            P(seq, head),
            P(seq, head),
            P(seq, head),
            P(),
            P(),
            P(seq, head),
            P(head),
        ),
        out_specs=P(seq, head),
        check_vma=False,
    )
```

```python
import jax
import jax.numpy as jnp
from jax import lax
from jax.experimental import pallas as pl
from jax.experimental.pallas import tpu as pltpu
from jax.sharding import Mesh
from jax.sharding import PartitionSpec as P

D = 5376
HEAD_DIM = 128
WINDOW = 1024
PATCH_SIDE = 64
POOL = 4
IMG_TOK = 256
Z = 16
ROWS_IN = 84
ROWS_OUT = 32
PAD_IN = 96
PAD_ALL = 144
WIDTH = 672

EPSILON = 1e-06
QUERY_SCALE = 168.0 ** (-0.5)
ROPE_BASE = 10000.0

GIVEN_SEQ = ("k", "a", "z")
GIVEN_HEAD = ("y", "core")
SEQ = ("k", "core", "z")
HEAD = ("y", "a")


def swapped(value):
    return lax.ppermute(value, ("a", "core"), [(0, 0), (1, 2), (2, 1), (3, 3)])


def from_half(value, flip):
    pairs = []
    for k in range(2):
        for a in range(2):
            for core in range(2):
                pairs.append(((k * 2 + a) * 2 + core, ((k ^ flip) * 2 + core) * 2 + a))
    return lax.ppermute(value, ("k", "a", "core"), pairs)


def shifted(value, steps):
    pairs = []
    for source in range(4 * Z):
        target = source + steps
        if 0 <= target < 4 * Z:
            place = [
                ((shard // (2 * Z)) * Z + shard % Z) * 2 + shard // Z % 2
                for shard in (source, target)
            ]
            pairs.append((place[0], place[1]))
    return lax.ppermute(value, ("k", "z", "core"), pairs)


def exchange(value, axes, count):
    spread = jnp.broadcast_to(value[None], (count, *value.shape))
    return lax.all_to_all(spread, axes, 0, 0, tiled=True)


def rms_scale(inputs, scale_gain):
    return (
        inputs * lax.rsqrt(jnp.mean(inputs * inputs, axis=-1, keepdims=True) + EPSILON) * scale_gain
    )


def image_of(positions, starts):
    inside = (positions[:, None] >= starts[None, :]) & (
        positions[:, None] < starts[None, :] + IMG_TOK
    )
    labels = jnp.arange(1, starts.shape[0] + 1, dtype=jnp.int32)
    return jnp.sum(jnp.where(inside, labels[None, :], 0), axis=1) - 1


def allowed_keys(query_pos, key_pos, starts, total_rows):
    query_img = image_of(query_pos, starts)
    key_img = image_of(key_pos, starts)
    inside = (key_pos >= 0) & (key_pos < total_rows)
    in_window = query_pos[:, None] - key_pos[None, :] < WINDOW
    causal = key_pos[None, :] <= query_pos[:, None]
    same_image = (query_img[:, None] == key_img[None, :]) & (query_img[:, None] >= 0)
    return inside[None, :] & in_window & (causal | same_image)


def attend(queries, key_rows, values, allowed):
    scores = jnp.einsum("qgrd,kgd->grqk", queries, key_rows, preferred_element_type=jnp.float32)
    scores = jnp.where(allowed[None, None], scores, -jnp.inf)
    row_max = jnp.max(scores, axis=-1, keepdims=True)
    weights = jnp.exp(scores - row_max)
    row_sum = jnp.sum(weights, axis=-1)
    mixed_heads = jnp.einsum(
        "grqk,kgd->qgrd", weights.astype(jnp.bfloat16), values, preferred_element_type=jnp.float32
    )
    return (mixed_heads / jnp.transpose(row_sum, (2, 0, 1))[..., None]).astype(jnp.bfloat16)


def add_part(whole_ref, gain_ref, weight_ref, block, start, squares):
    for shard in range(8):
        block[shard * ROWS_IN : (shard + 1) * ROWS_IN, :] = weight_ref[shard, 0, :ROWS_IN, :]
    part = whole_ref[0].astype(jnp.float32)
    gain = jnp.transpose(gain_ref[0])[:WIDTH, :1]
    scaled = (part * gain).astype(jnp.bfloat16)
    product = lax.dot_general(
        scaled, block[...], (((0,), (0,)), ((), ())), preferred_element_type=jnp.float32
    )
    return start + product, squares + jnp.sum(part * part, axis=0, keepdims=True)


def first_kernel(core_ref, whole_ref, gain_ref, weight_ref, total_ref, squares_ref, block):
    @pl.when(pl.program_id(0) == 0)
    def _():
        total_ref[...] = jnp.zeros_like(total_ref)
        squares_ref[...] = jnp.zeros_like(squares_ref)

    total_ref[...], squares_ref[...] = add_part(
        whole_ref, gain_ref, weight_ref, block, total_ref[...], squares_ref[...]
    )


def second_kernel(
    core_ref, whole_ref, gain_ref, weight_ref, start_ref, square_ref, cos_ref, sin_ref,
    query_gain_ref, key_gain_ref, query_ref, pair_ref, block, total, squares,
):
    step = pl.program_id(0)

    @pl.when(step == 0)
    def _():
        total[...] = start_ref[...]
        squares[...] = square_ref[...]

    total[...], squares[...] = add_part(
        whole_ref, gain_ref, weight_ref, block, total[...], squares[...]
    )

    @pl.when(step == pl.num_programs(0) - 1)
    def _():
        inverse = lax.rsqrt(squares[...] / D + EPSILON)
        inverse = jnp.transpose(jnp.broadcast_to(inverse, (HEAD_DIM, inverse.shape[1])))

        def head(index):
            return total[:, index * HEAD_DIM : (index + 1) * HEAD_DIM] * inverse

        def turned(rows, gain):
            mean_square = jnp.mean(rows * rows, axis=-1, keepdims=True)
            rows = rows * lax.rsqrt(mean_square + EPSILON) * gain
            return rows * cos_ref[...] + pltpu.roll(rows, HEAD_DIM // 2, 1) * sin_ref[...]

        for index in range(2):
            query_ref[:, index * HEAD_DIM : (index + 1) * HEAD_DIM] = (
                turned(head(index), query_gain_ref[...]) * QUERY_SCALE
            ).astype(jnp.bfloat16)
        pair_ref[:, :HEAD_DIM] = turned(head(2), key_gain_ref[...]).astype(jnp.bfloat16)
        pair_ref[:, HEAD_DIM:] = head(3).astype(jnp.bfloat16)


def own_block(step, core):
    return step // 2 * 4 + core[0] * 2 + step % 2


def other_block(step, core):
    return step // 2 * 4 + (1 - core[0]) * 2 + step % 2


def qkv_specs(block_of, width, rows):
    return [
        pl.BlockSpec((1, width, rows), lambda step, core: (block_of(step, core), 0, 0)),
        pl.BlockSpec((1, 8, 768), lambda step, core: (block_of(step, core), 0, 0)),
        pl.BlockSpec((8, 1, PAD_IN, 512), lambda step, core: (step % 2, step // 2, 0, 0)),
    ]


def project_first(core, whole, gain, weights):
    count, width, rows = whole.shape
    fixed = lambda step, core: (0, 0)
    return pl.pallas_call(
        first_kernel,
        grid_spec=pltpu.PrefetchScalarGridSpec(
            num_scalar_prefetch=1,
            grid=(count // 2,),
            in_specs=qkv_specs(own_block, width, rows),
            out_specs=[pl.BlockSpec((rows, 512), fixed), pl.BlockSpec((1, rows), fixed)],
            scratch_shapes=[pltpu.VMEM((width, 512), jnp.bfloat16)],
        ),
        out_shape=[
            jax.ShapeDtypeStruct((rows, 512), jnp.float32),
            jax.ShapeDtypeStruct((1, rows), jnp.float32),
        ],
        compiler_params=pltpu.CompilerParams(vmem_limit_bytes=24 * 2**20),
        cost_estimate=pl.CostEstimate(
            flops=rows * 512 * D, bytes_accessed=5 * 2**20, transcendentals=0
        ),
    )(core, whole, gain, weights)


def project_second(
    core, whole, gain, weights, total, squares, cosine, sine, query_gain, key_gain
):
    count, width, rows = whole.shape
    fixed = lambda step, core: (0, 0)
    return pl.pallas_call(
        second_kernel,
        grid_spec=pltpu.PrefetchScalarGridSpec(
            num_scalar_prefetch=1,
            grid=(count // 2,),
            in_specs=qkv_specs(other_block, width, rows)
            + [
                pl.BlockSpec((rows, 512), fixed),
                pl.BlockSpec((1, rows), fixed),
                pl.BlockSpec((rows, HEAD_DIM), fixed),
                pl.BlockSpec((rows, HEAD_DIM), fixed),
                pl.BlockSpec((1, HEAD_DIM), fixed),
                pl.BlockSpec((1, HEAD_DIM), fixed),
            ],
            out_specs=[pl.BlockSpec((rows, 256), fixed), pl.BlockSpec((rows, 256), fixed)],
            scratch_shapes=[
                pltpu.VMEM((width, 512), jnp.bfloat16),
                pltpu.VMEM((rows, 512), jnp.float32),
                pltpu.VMEM((1, rows), jnp.float32),
            ],
        ),
        out_shape=[
            jax.ShapeDtypeStruct((rows, 256), jnp.bfloat16),
            jax.ShapeDtypeStruct((rows, 256), jnp.bfloat16),
        ],
        compiler_params=pltpu.CompilerParams(vmem_limit_bytes=24 * 2**20),
        cost_estimate=pl.CostEstimate(
            flops=rows * 512 * D, bytes_accessed=5 * 2**20, transcendentals=0
        ),
    )(
        core, whole, gain, weights, total, squares, cosine, sine,
        query_gain[None, :], key_gain[None, :],
    )


def out_kernel(
    core_ref, own_ref, other_ref, along_ref, across_ref, result_ref, squares_ref, total
):
    step = pl.program_id(0)

    @pl.when(step == 0)
    def _():
        total[...] = jnp.zeros_like(total)

    for heads_ref, weight_ref in ((own_ref, along_ref), (other_ref, across_ref)):
        left = weight_ref[:, 0, :ROWS_OUT, :].reshape(8 * ROWS_OUT, 512)
        right = weight_ref[:, 0, ROWS_OUT:, :]
        right = jnp.concatenate([right[:, :, :256], right[:, :, 256:]], axis=1)
        right = right.reshape(8 * ROWS_OUT, 256)
        heads = heads_ref[0]
        for first, part in ((0, left), (512, right)):
            total[first : first + part.shape[1], :] += lax.dot_general(
                part, heads, (((0,), (0,)), ((), ())), preferred_element_type=jnp.float32
            )

    @pl.when(step == pl.num_programs(0) - 1)
    def _():
        result = total[:WIDTH, :]
        result_ref[...] = result.astype(jnp.bfloat16)
        squares = jnp.sum(result * result, axis=0, keepdims=True)
        squares_ref[...] = jnp.broadcast_to(squares[None], squares_ref.shape)


def project_out(core, heads, along, across):
    count, depth, rows = heads.shape
    fixed = lambda step, core: (0, 0)
    weights = pl.BlockSpec(
        (8, 1, PAD_ALL - PAD_IN, 512), lambda step, core: (step % 2, step // 2, 2, 0)
    )
    return pl.pallas_call(
        out_kernel,
        grid_spec=pltpu.PrefetchScalarGridSpec(
            num_scalar_prefetch=1,
            grid=(count // 2,),
            in_specs=[
                pl.BlockSpec((1, depth, rows), lambda step, core: (own_block(step, core), 0, 0)),
                pl.BlockSpec((1, depth, rows), lambda step, core: (other_block(step, core), 0, 0)),
                weights,
                weights,
            ],
            out_specs=[
                pl.BlockSpec((WIDTH, rows), fixed),
                pl.BlockSpec((16, 1, rows), lambda step, core: (0, 0, 0)),
            ],
            scratch_shapes=[pltpu.VMEM((768, rows), jnp.float32)],
        ),
        out_shape=[
            jax.ShapeDtypeStruct((WIDTH, rows), jnp.bfloat16),
            jax.ShapeDtypeStruct((16, 1, rows), jnp.float32),
        ],
        compiler_params=pltpu.CompilerParams(vmem_limit_bytes=24 * 2**20),
        cost_estimate=pl.CostEstimate(
            flops=2 * rows * 768 * 2048, bytes_accessed=5 * 2**20, transcendentals=0
        ),
    )(core, heads, heads, along, across)


def body(
    tokens,
    features,
    starts,
    sources,
    soft_gain,
    proj_weight,
    input_gain,
    query_weight,
    key_weight,
    value_weight,
    query_gain,
    key_gain,
    out_weight,
    post_gain,
):
    tok_rows, width = tokens.shape
    head_count = 8
    x_count = 4
    seq_count = x_count * Z
    core_index = lax.axis_index("core")
    z_index = lax.axis_index("z")
    seq_index = lax.axis_index(SEQ)
    total_rows = seq_count * tok_rows

    out_right = jnp.pad(out_weight[:, 512:], ((0, 0), (0, 768 - width)))
    local = jnp.concatenate(
        [
            jnp.pad(
                jnp.concatenate([query_weight, key_weight, value_weight], axis=1),
                ((0, PAD_IN - ROWS_IN), (0, 0)),
            ),
            out_weight[:, :512],
            jnp.concatenate([out_right[:16], out_right[16:]], axis=1),
        ],
        axis=0,
    )
    same_half = from_half(local, 0)
    other_half = from_half(local, 1)
    k_first = lax.axis_index("k") == 0
    both = jnp.stack(
        [
            jnp.where(k_first, same_half, other_half),
            jnp.where(k_first, other_half, same_half),
        ]
    )
    core = core_index.astype(jnp.int32)[None]

    image_count = starts.shape[0]
    vis = features.shape[2]
    pooled_side = PATCH_SIDE // POOL
    pool_rows = features.shape[0] // POOL
    block_rows = pool_rows * pooled_side
    shards_each = pooled_side // pool_rows
    row = jnp.arange(block_rows, dtype=jnp.int32)
    patch = jnp.arange(features.shape[0] * PATCH_SIDE, dtype=jnp.int32)
    square = patch // (PATCH_SIDE * POOL) * pooled_side + patch % PATCH_SIDE // POOL
    ones = (row[:, None] == square[None, :]).astype(jnp.bfloat16)
    pooled = jnp.dot(
        ones, features.reshape(-1, vis), preferred_element_type=jnp.float32
    ) / (POOL * POOL)
    soft = rms_scale(pooled, soft_gain).astype(jnp.bfloat16)
    vis_part = vis // head_count
    soft_part = lax.dynamic_slice_in_dim(
        soft, lax.axis_index(GIVEN_HEAD) * vis_part, vis_part, 1
    )
    target = jnp.arange(8, dtype=jnp.int32)
    target_k, target_a, target_core = target // 4, target // 2 % 2, target % 2
    target_seq = (target_k * 2 + target_core) * Z + z_index
    frame_pos = (
        target_seq[:, None] * tok_rows + jnp.arange(tok_rows, dtype=jnp.int32)[None, :]
    ).reshape(-1)
    frame_image = image_of(frame_pos, starts)
    row_base = sources // shards_each * (block_rows * shards_each) - starts
    image_ids = jnp.arange(image_count, dtype=jnp.int32)
    frame_row = jnp.sum(
        jnp.where(frame_image[:, None] == image_ids[None, :], row_base[None, :], 0), axis=1
    )
    wanted = (frame_image >= 0) & jnp.repeat(target_a == core_index, tok_rows)
    frame_row = jnp.where(wanted, frame_row + frame_pos, -1)
    x_index = lax.axis_index(("k", "a"))
    here = x_index * (Z * block_rows) + jnp.arange(Z * block_rows, dtype=jnp.int32)
    soft_z = exchange(soft_part, "z", Z).reshape(Z * block_rows, vis_part)
    tokens = swapped(tokens)
    soft_z, both, tokens, proj_weight = lax.optimization_barrier(
        (soft_z, both, tokens, proj_weight)
    )
    along = lax.all_gather(both, "z", axis=0)
    proj_other = lax.ppermute(proj_weight, ("a", "core"), [(0, 1), (3, 2)])
    proj_weight = jnp.where(core_index == lax.axis_index("a"), proj_weight, proj_other)
    chosen = (frame_row[:, None] == here[None, :]).astype(jnp.bfloat16)
    chosen = chosen.reshape(8, tok_rows, Z * block_rows)
    frames = jnp.einsum("sk,xps->xkp", soft_z, chosen, preferred_element_type=jnp.float32)
    frames = lax.all_to_all(
        frames.astype(jnp.bfloat16), ("k", "a", "core"), 0, 0, tiled=True
    )
    mine = jnp.sum(frames.astype(jnp.float32), axis=0).astype(jnp.bfloat16)
    soft_rows = exchange(mine, HEAD, head_count).reshape(vis, tok_rows)
    gain_parts = jnp.broadcast_to(
        jnp.pad(input_gain.reshape(head_count, 1, width), ((0, 0), (0, 0), (0, 768 - width))),
        (head_count, 8, 768),
    )
    embedded = lax.dot_general(
        proj_weight, soft_rows, (((0,), (0,)), ((), ())),
        preferred_element_type=jnp.float32,
    ).astype(jnp.bfloat16)
    my_pos = seq_index * tok_rows + jnp.arange(tok_rows, dtype=jnp.int32)
    my_image = image_of(my_pos, starts)
    residual = jnp.where((my_image >= 0)[None, :], embedded, tokens.T)

    whole = exchange(residual, HEAD, head_count)
    given_residual = swapped(residual)
    along, whole, given_residual = lax.optimization_barrier((along, whole, given_residual))
    across = lax.ppermute(along, "core", [(0, 1), (1, 0)])
    half = HEAD_DIM // 2
    frequency = ROPE_BASE ** (-jnp.arange(half, dtype=jnp.float32) * 2.0 / HEAD_DIM)
    angles = my_pos.astype(jnp.float32)[:, None] * frequency[None, :]
    cosine, sine = jnp.cos(angles), jnp.sin(angles)
    total, row_squares = project_first(core, whole, gain_parts, along)
    queries, own = project_second(
        core,
        whole,
        gain_parts,
        across,
        total,
        row_squares,
        jnp.concatenate([cosine, cosine], axis=1),
        jnp.concatenate([-sine, sine], axis=1),
        query_gain,
        key_gain,
    )
    past_count = WINDOW // tok_rows
    near = jnp.concatenate([shifted(own, 2), shifted(own, 1)], axis=0)
    near, later = lax.optimization_barrier((near, shifted(own, -1)))
    window = jnp.concatenate([shifted(near, 2), near, own, later], axis=0)
    key_pos = (seq_index - past_count) * tok_rows + jnp.arange(window.shape[0], dtype=jnp.int32)
    allowed = allowed_keys(my_pos, key_pos, starts, total_rows)
    attended = attend(
        queries.reshape(tok_rows, 1, 2, HEAD_DIM),
        window[:, :HEAD_DIM].reshape(-1, 1, HEAD_DIM),
        window[:, HEAD_DIM:].reshape(-1, 1, HEAD_DIM),
        allowed,
    )
    attended = attended.reshape(tok_rows, 2 * HEAD_DIM).T
    heads_all = exchange(attended, HEAD, head_count)
    projected, squares = project_out(core, heads_all, along, across)
    given = swapped(projected).astype(jnp.float32)
    all_squares = lax.all_to_all(squares, ("a", "y", "core"), 0, 0, tiled=True)
    all_squares = all_squares.reshape(8, 2, tok_rows)
    from_core = jnp.arange(2, dtype=jnp.int32) == lax.axis_index("a")
    squares = jnp.sum(jnp.where(from_core[None, :, None], all_squares, 0.0), axis=(0, 1))
    post = given * lax.rsqrt(squares[None, :] / D + EPSILON) * post_gain[:, None]
    return (given_residual.astype(jnp.float32) + post).astype(jnp.bfloat16).T


def solution(mesh):
    split = Mesh(mesh.devices.reshape(2, 2, Z, 4, 2), ("k", "a", "z", "y", "core"))
    seq, head = GIVEN_SEQ, GIVEN_HEAD
    return jax.shard_map(
        body,
        mesh=split,
        in_specs=(
            P(seq, head),
            P(seq, None, None),
            P(),
            P(),
            P(),
            P(None, head),
            P(),
            P(seq, head),
            P(seq, head),
            P(seq, head),
            P(),
            P(),
            P(seq, head),
            P(head),
        ),
        out_specs=P(seq, head),
        check_vma=False,
    )
```
